256 devices in a mesh: branch: 32 (over z, x), head: 8 (over y, core).
Axes of the slice: x: 4, y: 4, z: 8, core: 2. Of those that a mesh axis runs over, the one named last changes fastest.
Arguments:
- query_nope: bfloat16 [3072, 16384], P('branch', 'head'), may hold values from -6 to 6
- query_rope: bfloat16 [3072, 8192], P('branch', 'head'), may hold values from -448 to 448
- key_up: bfloat16 [128, 128, 512], P('head'), may hold values from -0.5 to 0.5
- value_up: bfloat16 [128, 512, 128], P('head'), may hold values from -1.5 to 1.5
- out_weight: bfloat16 [16384, 7168], P('head', 'branch'), may hold values from -0.046875 to 0.046875
- block_pool: bfloat16 [768, 128, 576], P('branch'), may hold values from -6 to 6
- recent_blocks: bfloat16 [768, 128, 576], P('branch'), may hold values from -6 to 6
- new_latent: bfloat16 [3072, 576], P('branch'), may hold values from -6 to 6
- parent: int32 [768], P('branch'), may hold values from 0 to 767, as said below
- lengths: int32 [768], P('branch'), may hold values from 1 to 128
- block_table: int32 [768, 1], P('branch'), may hold values from 0 to 23, as said below
Outputs:
- mixed: bfloat16 [3072, 7168], P('head', 'branch')
The draws below stay inside these ranges and needn't reach their ends.
Inputs may be any that keep to these rules, and one draw needn't show every extreme that they name: Children 2i and 2i+1 share one parent; of the 12 sibling pairs of one device at most 1 have parents on one device, and on every device some source device holds exactly 1 of its pairs' parents. Entries name pool blocks of the child's own device: block j of child b is block_pool row 24 * (b // 24) + block_table[b, j].
All inputs are finite; a program needn't handle non-finite values.
Results may differ from the reference program's by a relative error of at most 0.014.
Values may be sent and summed in bfloat16 or wider, within the bound.
A program may use at most 128 MiB of HBM per device.

```python
import jax
import jax.numpy as jnp
from jax import lax

D = 7168
HEADS = 128
NOPE = 128
ROPE = 64
LAT = 512
VDIM = 128
BLOCK = 128
STEPS = 4
B_DEV = 24
LOC = 1
BRANCHES = 768
ROWS = 3072


def shared_parts(key):
    latent_rows = jax.random.normal(jax.random.fold_in(key, 101), (BRANCHES * STEPS, LAT + ROPE), jnp.float32)
    latent_rows = jnp.clip(latent_rows, -5.5, 5.5)
    return latent_rows


def draw_query_rope(key, part):
    latent_rows = shared_parts(key)
    key = jax.random.fold_in(key, 2)
    noise = jnp.clip(jax.random.normal(key, (BRANCHES * STEPS, HEADS, ROPE), jnp.float32), -5.0, 5.0)
    values = noise + 0.8 * latent_rows[:, None, LAT:]
    return values.reshape(BRANCHES * STEPS, HEADS * ROPE).astype(jnp.bfloat16)


def draw_new_latent(key, part):
    latent_rows = shared_parts(key)
    return latent_rows.astype(jnp.bfloat16)


def draw_parent(key, part):
    key = jax.random.fold_in(key, 3)
    groups = BRANCHES // B_DEV
    pair_count = B_DEV // 2
    sub_keys = jax.random.split(jax.random.fold_in(key, 1), groups)
    shuffled = jax.vmap(lambda sub_key: jax.random.permutation(sub_key, groups))(sub_keys).astype(jnp.int32)
    first_row = shuffled[0]
    first_row = jnp.where(first_row == groups - 1, first_row[0], first_row).at[0].set(groups - 1)
    last_row = shuffled[groups - 1]
    last_row = jnp.where(last_row == 0, last_row[0], last_row).at[0].set(0)
    shuffled = shuffled.at[0].set(first_row).at[groups - 1].set(last_row)
    pick = jnp.arange(pair_count, dtype=jnp.int32) % groups
    sources = shuffled[:, pick]
    within = jax.random.randint(jax.random.fold_in(key, 2), (groups, pair_count), 0, B_DEV)
    within = within.at[0, 0].set(B_DEV - 1).at[groups - 1, 0].set(0)
    parents = sources * B_DEV + within
    return jnp.repeat(parents[:, :, None], 2, axis=2).reshape(BRANCHES).astype(jnp.int32)


def draw_lengths(key, part):
    key = jax.random.fold_in(key, 4)
    drawn_rows = jax.random.randint(key, (BRANCHES,), 1, LOC * BLOCK + 1)
    return drawn_rows.at[0].set(LOC * BLOCK).at[1].set(1).astype(jnp.int32)


def draw_block_table(key, part):
    key = jax.random.fold_in(key, 5)
    drawn_rows = jax.random.randint(key, (BRANCHES, LOC), 0, B_DEV * LOC)
    return drawn_rows.at[0, 0].set(B_DEV * LOC - 1).at[1, 0].set(0).astype(jnp.int32)


def block_levels(stream_key, dims, pieces, smallest, high):
    def one(dim, blocks):
        draws = jax.random.uniform(jax.random.fold_in(jax.random.fold_in(stream_key, 6), dim), (blocks,), jnp.float32, smallest / len(pieces), high / len(pieces))
        return jnp.repeat(jnp.exp(draws), dims[dim] // blocks).reshape((-1,) + (1,) * (len(dims) - dim - 1))

    loudness = one(*pieces[0])
    for cut in pieces[1:]:
        loudness = loudness * one(*cut)
    return loudness


def normal_values(key, extent, scale, reach, shards=(), held_as=jnp.bfloat16):
    drawn = scale * jax.random.normal(key, extent, jnp.float32)
    if shards:
        drawn = drawn * block_levels(key, extent, shards, -0.22, 0.18)
    return jnp.clip(drawn, -reach, reach).astype(held_as)


def setup_inputs(seed: int = 0) -> dict:
    key_of = jax.random.split(jax.random.key(seed), 12)
    query_nope = normal_values(key_of[0], (ROWS, HEADS * NOPE), 1.0, 6.0, ((0, 32), (1, 8)))
    query_rope = draw_query_rope(jax.random.fold_in(key_of[11], 71), 0)
    key_up = normal_values(key_of[2], (HEADS, NOPE, LAT), NOPE ** -0.5, 0.5, ((0, 8),))
    value_up = normal_values(key_of[3], (HEADS, LAT, VDIM), (LAT // 32) ** -0.5, 1.5, ((0, 8),))
    out_weight = normal_values(key_of[4], (HEADS * VDIM, D), (HEADS * VDIM) ** -0.5, 0.046875, ((0, 8), (1, 32)))
    block_pool = normal_values(key_of[5], (BRANCHES * LOC, BLOCK, LAT + ROPE), 1.0, 6.0, ((0, 32),))
    recent_blocks = normal_values(key_of[6], (BRANCHES, BLOCK, LAT + ROPE), 1.0, 6.0, ((0, 32),))
    new_latent = draw_new_latent(jax.random.fold_in(key_of[11], 71), 0)
    parent = draw_parent(jax.random.fold_in(key_of[11], 71), 0)
    lengths = draw_lengths(jax.random.fold_in(key_of[11], 71), 0)
    block_table = draw_block_table(jax.random.fold_in(key_of[11], 71), 0)
    return dict(query_nope=query_nope, query_rope=query_rope, key_up=key_up, value_up=value_up, out_weight=out_weight, block_pool=block_pool, recent_blocks=recent_blocks, new_latent=new_latent, parent=parent, lengths=lengths, block_table=block_table)


def reference(query_nope, query_rope, key_up, value_up, out_weight, block_pool, recent_blocks, new_latent, parent, lengths, block_table):
    width = LAT + ROPE
    score_scale = (NOPE + ROPE) ** -0.5
    key_count = (LOC + 1) * BLOCK + STEPS
    q_heads = query_nope.reshape(ROWS, HEADS, NOPE).astype(jnp.float32)
    q_latent = jnp.einsum("rhn,hnl->rhl", q_heads, key_up.astype(jnp.float32)).astype(jnp.bfloat16)
    query_vectors = jnp.concatenate([q_latent, query_rope.reshape(ROWS, HEADS, ROPE)], axis=2)
    query_vectors = query_vectors.reshape(BRANCHES, STEPS, HEADS, width)
    pool_base = (jnp.arange(BRANCHES, dtype=jnp.int32) // B_DEV) * (B_DEV * LOC)
    position = jnp.arange(key_count, dtype=jnp.int32)
    fresh_index = position - (LOC + 1) * BLOCK
    step_index = jnp.arange(STEPS, dtype=jnp.int32)

    def attend(branch):
        prefix_latent = block_pool[pool_base[branch] + block_table[branch]].reshape(LOC * BLOCK, width)
        forked_rows = recent_blocks[parent[branch]]
        newly_drafted_keys = lax.dynamic_slice_in_dim(new_latent, branch * STEPS, STEPS, 0)
        key_rows = jnp.concatenate([prefix_latent, forked_rows, newly_drafted_keys], axis=0)
        scores = jnp.einsum("thc,kc->thk", query_vectors[branch].astype(jnp.float32), key_rows.astype(jnp.float32)) * score_scale
        allow_prefix = (position < LOC * BLOCK) & (position < lengths[branch])
        allow_fork = (position >= LOC * BLOCK) & (position < (LOC + 1) * BLOCK)
        allow_fresh = (fresh_index >= 0)[None, :] & (fresh_index[None, :] <= step_index[:, None])
        allowed = (allow_prefix | allow_fork)[None, :] | allow_fresh
        scores = jnp.where(allowed[:, None, :], scores, -jnp.inf)
        row_peak = jnp.max(scores, axis=2, keepdims=True)
        weights = jnp.exp(scores - row_peak).astype(jnp.bfloat16)
        weight_sum = jnp.sum(weights.astype(jnp.float32), axis=2)
        context_vectors = jnp.einsum("thk,kl->thl", weights.astype(jnp.float32), key_rows[:, :LAT].astype(jnp.float32))
        return (context_vectors / weight_sum[:, :, None]).astype(jnp.bfloat16)

    contexts = lax.map(attend, jnp.arange(BRANCHES, dtype=jnp.int32)).reshape(ROWS, HEADS, LAT)
    attended = jnp.einsum("rhl,hlv->rhv", contexts.astype(jnp.float32), value_up.astype(jnp.float32))
    attended = attended.astype(jnp.bfloat16).reshape(ROWS, HEADS * VDIM)
    return jnp.dot(attended, out_weight, preferred_element_type=jnp.float32).astype(jnp.bfloat16)
```

```python
import functools

import jax
import jax.numpy as jnp
from jax import lax
from jax.experimental import pallas as pl
from jax.experimental.pallas import tpu as pltpu
from jax.sharding import PartitionSpec as P

NOPE = 128
ROPE = 64
LAT = 512
VDIM = 128
BLOCK = 128
STEPS = 4
B_DEV = 24
PAIRS = B_DEV // 2
WIDTH = LAT + ROPE
HEADS = 16
ROWS = B_DEV * STEPS
HALF = ROWS // 2
QROWS = ROWS * HEADS
COLS = 224
NZ, NX, NY = 8, 4, 4
GROUPS = NZ * NX
PART = 80
LANES = LAT // 128
SCALE = (NOPE + ROPE) ** -0.5
BF = jnp.bfloat16
F32 = jnp.float32
MESH = pl.DeviceIdType.MESH
NT = (((1,), (1,)), ((), ()))


def dot(a, b):
    return jnp.dot(a, b, preferred_element_type=F32)


def dot_nt(a, b):
    return lax.dot_general(a, b, NT, preferred_element_type=F32)


def remote(src, dst, send, recv, **where):
    return pltpu.make_async_remote_copy(
        src_ref=src, dst_ref=dst, send_sem=send, recv_sem=recv,
        device_id=where, device_id_type=MESH,
    )


def attend_kernel(
    par, lens, table,
    qn_hbm, qr_hbm, ku_hbm, vu_hbm, pool_hbm, recent_hbm, nl_hbm,
    att,
    qn, qr, ku, vu, pool, nl, nlt,
    qs, ctx, peak, total,
    mine, packed, slots, my_par, all_par, pick_v, pick_s, parts, fork,
    load_sem, pick_sem, par_send, par_recv, out_send, out_recv, ring_send, ring_recv, core_send, core_recv,
):
    me = lax.axis_index("branch")
    head = lax.axis_index("head")
    y, core = head // 2, lax.rem(head, 2)
    up, down = lax.rem(y + 1, NY), lax.rem(y + 3, NY)
    far = lax.rem(y + 2, NY)
    row0 = pl.multiple_of(y * 144 + core * 64, 16)

    loads = [
        pltpu.make_async_copy(recent_hbm.at[:, pl.ds(row0, PART), :], mine, load_sem.at[0]),
        pltpu.make_async_copy(ku_hbm, ku, load_sem.at[1]),
        pltpu.make_async_copy(qn_hbm, qn, load_sem.at[2]),
        pltpu.make_async_copy(pool_hbm, pool, load_sem.at[3]),
        pltpu.make_async_copy(qr_hbm, qr, load_sem.at[4]),
        pltpu.make_async_copy(nl_hbm, nl, load_sem.at[5]),
        pltpu.make_async_copy(vu_hbm, vu, load_sem.at[6]),
    ]
    for load in loads:
        load.start()

    barrier = pltpu.get_barrier_semaphore()

    def greet(i, _):
        pl.semaphore_signal(barrier, inc=1, device_id={"branch": lax.rem(me + i, GROUPS)}, device_id_type=MESH)
        return 0

    lax.fori_loop(1, GROUPS, greet, 0)
    for other in (up * 2 + core, down * 2 + core, y * 2 + 1 - core):
        pl.semaphore_signal(barrier, inc=1, device_id={"head": other}, device_id_type=MESH)

    lane = lax.broadcasted_iota(jnp.int32, (1, 128), 1)
    row = jnp.zeros((1, 128), jnp.int32) - 1
    for b in range(0, B_DEV, 2):
        row = jnp.where(lane == b, par[b], row)
    my_par[...] = row
    all_par[me] = row
    pl.semaphore_wait(barrier, GROUPS - 1 + 3)

    def par_copy(i):
        d = lax.rem(me + i, GROUPS)
        return remote(my_par, all_par.at[me], par_send.at[i], par_recv.at[me], branch=d)

    def start_par(i, _):
        par_copy(i).start()
        return 0

    lax.fori_loop(1, GROUPS, start_par, 0)

    loads[1].wait()
    loads[2].wait()
    for h in range(HEADS):
        q = dot(qn[:, h * NOPE:(h + 1) * NOPE], ku[h])
        q = q.astype(BF).astype(F32)
        for j in range(LANES):
            qs[j, pl.ds(h, ROWS, stride=HEADS), :] = q[:, j * 128:(j + 1) * 128]

    def wait_par(i, _):
        src = lax.rem(me + i, GROUPS)
        remote(my_par, all_par.at[src], par_send.at[i], par_recv.at[src], branch=src).wait()
        return 0

    lax.fori_loop(1, GROUPS, wait_par, 0)
    local = all_par[...] - me * B_DEV
    hit = (local >= 0) & (local < B_DEV)
    pick_v[...] = jnp.broadcast_to(
        jnp.sum(jnp.where(hit, local, 0), axis=2, keepdims=True), (GROUPS, 1, 128)
    )
    pick = pltpu.make_async_copy(pick_v, pick_s, pick_sem)
    pick.start()
    loads[0].wait()
    pick.wait()

    def send_block(i, _):
        d = lax.rem(me + i, GROUPS)
        packed[d] = mine[pick_s[d, 0, 0]]
        remote(packed.at[d], slots.at[me], out_send.at[d], out_recv.at[me], branch=d).start()
        return 0

    lax.fori_loop(1, GROUPS, send_block, 0)
    slots[me] = mine[pick_s[me, 0, 0]]

    loads[3].wait()
    loads[4].wait()
    loads[5].wait()
    nlt[...] = jnp.zeros_like(nlt)
    nlt[:, :ROWS] = nl[...].astype(F32).T.astype(BF)

    key = lax.broadcasted_iota(jnp.int32, (STEPS * HEADS, 256), 1)
    step = lax.broadcasted_iota(jnp.int32, (STEPS * HEADS, 256), 0) // HEADS

    def query(rows):
        return jnp.concatenate([qs[j, rows, :] for j in range(LANES)], axis=1).astype(BF)

    def prefix(b, _):
        rows = pl.ds(pl.multiple_of(b * 64, 64), 64)
        keys = jnp.concatenate([pool[table[b]], nlt[...]], axis=1)
        s = dot(query(rows), keys[:LAT]) + dot(qr[rows, :], keys[LAT:])
        fresh = key - BLOCK - b * STEPS
        allowed = (key < lens[b]) | ((fresh >= 0) & (fresh <= step))
        s = jnp.where(allowed, s * SCALE, -jnp.inf)
        m = jnp.max(s, axis=1, keepdims=True)
        w = jnp.exp(s - m).astype(BF)
        total[rows, :] = jnp.broadcast_to(jnp.sum(w.astype(F32), axis=1, keepdims=True), (64, 128))
        peak[rows, :] = jnp.broadcast_to(m, (64, 128))
        c = dot_nt(w, keys[:LAT])
        for j in range(LANES):
            ctx[j, rows, :] = c[:, j * 128:(j + 1) * 128]
        return 0

    lax.fori_loop(0, B_DEV // 2, prefix, 0)

    def wait_block(i, _):
        src = lax.rem(me + i, GROUPS)
        remote(packed.at[src], slots.at[src], out_send.at[src], out_recv.at[src], branch=src).wait()
        return 0

    lax.fori_loop(1, GROUPS, wait_block, 0)
    for p in range(PAIRS):
        parts[head, p] = slots[par[2 * p] // B_DEV]

    def piece(h, half):
        at = parts.at[h]
        return at if half is None else at.at[pl.ds(half * (PAIRS // 2), PAIRS // 2)]

    def ring(n, h, half, to):
        return remote(piece(h, half), piece(h, half), ring_send.at[n], ring_recv.at[n], head=to * 2 + core)

    def swap(n, h, half):
        return remote(piece(h, half), piece(h, half), core_send.at[n], core_recv.at[n], head=y * 2 + 1 - core)

    ring(0, head, None, up).start()
    ring(1, head, None, down).start()
    swap(0, head, None).start()

    lax.fori_loop(B_DEV // 2, B_DEV * 3 // 4, prefix, 0)

    from_down, from_up, from_far = down * 2 + core, up * 2 + core, far * 2 + core
    ring(0, from_down, None, up).wait()
    ring(2, from_down, 0, up).start()
    swap(1, from_down, None).start()
    ring(1, from_up, None, down).wait()
    ring(3, from_up, 1, down).start()
    swap(2, from_up, None).start()

    lax.fori_loop(B_DEV * 3 // 4, B_DEV, prefix, 0)

    ring(2, from_far, 0, up).wait()
    swap(3, from_far, 0).start()
    ring(3, from_far, 1, down).wait()
    swap(4, from_far, 1).start()
    other = 1 - core
    swap(0, y * 2 + other, None).wait()
    swap(1, down * 2 + other, None).wait()
    swap(2, up * 2 + other, None).wait()
    swap(3, far * 2 + other, 0).wait()
    swap(4, far * 2 + other, 1).wait()

    def gather(p, _):
        for yy in range(NY):
            fork[p, yy * 144:yy * 144 + 80] = parts[2 * yy, p]
            fork[p, yy * 144 + 80:yy * 144 + 144] = parts[2 * yy + 1, p, 16:80]
        return 0

    lax.fori_loop(0, PAIRS, gather, 0)

    def forked(p, _):
        rows = pl.ds(pl.multiple_of(p * 128, 128), 128)
        keys = fork[p]
        s = dot(query(rows), keys[:LAT]) + dot(qr[rows, :], keys[LAT:])
        s = s * SCALE
        old = peak[rows, :][:, :1]
        m = jnp.maximum(jnp.max(s, axis=1, keepdims=True), old)
        w = jnp.exp(s - m).astype(BF)
        back = jnp.exp(old - m)
        norm = total[rows, :][:, :1] * back + jnp.sum(w.astype(F32), axis=1, keepdims=True)
        c = dot_nt(w, keys[:LAT])
        scale = 1.0 / norm
        for j in range(LANES):
            both = (ctx[j, rows, :] * back + c[:, j * 128:(j + 1) * 128]) * scale
            ctx[j, rows, :] = both.astype(BF).astype(F32)
        return 0

    lax.fori_loop(0, PAIRS, forked, 0)
    loads[6].wait()
    for h in range(HEADS):
        c = [ctx[j, pl.ds(h, ROWS, stride=HEADS), :] for j in range(LANES)]
        c = jnp.concatenate(c, axis=1).astype(BF)
        att[:, h * VDIM:(h + 1) * VDIM] = dot(c, vu[h]).astype(BF)


def project_kernel(
    att, wt, out,
    held, made, landed, cut, final,
    z_send, z_recv, r_send, r_recv, x_send, x_recv,
):
    me = lax.axis_index("branch")
    head = lax.axis_index("head")
    z, x = me // NX, lax.rem(me, NX)
    nxt = lax.rem(z + 1, NZ) * NX + x
    prv = lax.rem(z + NZ - 1, NZ) * NX + x

    barrier = pltpu.get_barrier_semaphore()
    for other in (nxt, prv):
        pl.semaphore_signal(barrier, inc=1, device_id={"branch": other}, device_id_type=MESH)
    for i in range(1, NX):
        pl.semaphore_signal(barrier, inc=1, device_id={"branch": z * NX + lax.rem(x + i, NX)}, device_id_type=MESH)
    for i in range(1, 8):
        pl.semaphore_signal(barrier, inc=1, device_id={"head": lax.rem(head + i, 8)}, device_id_type=MESH)
    pl.semaphore_wait(barrier, 2 + 3 + 7)

    def half(slot, s):
        if slot == 0:
            return att.at[pl.ds(s * HALF, HALF)]
        return held.at[slot, pl.ds(s * HALF, HALF)]

    def hop(way, k, s):
        came, goes = (k - 1, k) if way == 0 else ((9 - k) % 8, 8 - k)
        return remote(
            half(came, s), half(goes, s), z_send.at[way, k - 1, s], z_recv.at[way, k - 1, s],
            branch=nxt if way == 0 else prv,
        )

    hops = []

    def go(way, k, s):
        c = hop(way, k, s)
        c.start()
        hops.append(c)

    def reduce_copy(slot):
        return remote(made.at[slot], landed.at[head], r_send.at[slot], r_recv.at[head], head=lax.rem(z + 8 - slot, 8))

    def multiply(slot):
        a = att[...] if slot == 0 else held[slot]
        made[slot] = dot_nt(a, wt[...]).astype(BF)

        @pl.when(lax.rem(z + 8 - slot, 8) != head)
        def _():
            reduce_copy(slot).start()

    for s in (0, 1):
        go(0, 1, s)
        go(1, 1, s)
    multiply(0)
    for k in (1, 2, 3):
        for s in (0, 1):
            for way in (0, 1):
                t = s if way == 0 else 1 - s
                hop(way, k, t).wait_recv()
                if k < 3 or t == way:
                    go(way, k + 1, t)
        multiply(k)
        multiply(8 - k)
    hop(0, 4, 0).wait_recv()
    hop(1, 4, 1).wait_recv()
    multiply(4)

    acc = made[lax.rem(z + 8 - head, 8)].astype(F32)
    for i in range(1, 8):
        src = lax.rem(head + i, 8)
        remote(made.at[0], landed.at[src], r_send.at[0], r_recv.at[src], head=src).wait_recv()
        acc = acc + landed[src].astype(F32)
    acc = acc.astype(BF)
    for i in range(NX):
        cut[i] = acc[:, i * COLS:(i + 1) * COLS]
    final[x] = cut[x]
    spread = []
    for i in range(1, NX):
        d = lax.rem(x + i, NX)
        c = remote(cut.at[d], final.at[x], x_send.at[i], x_recv.at[x], branch=z * NX + d)
        c.start()
        spread.append(c)
    for i in range(1, NX):
        d = lax.rem(x + i, NX)
        remote(cut.at[d], final.at[d], x_send.at[i], x_recv.at[d], branch=z * NX + d).wait_recv()
    for i in range(NX):
        out[i * ROWS:(i + 1) * ROWS, :] = final[i]

    for c in hops:
        c.wait_send()
    for c in spread:
        c.wait_send()
    for slot in range(8):

        @pl.when(lax.rem(z + 8 - slot, 8) != head)
        def _(slot=slot):
            reduce_copy(slot).wait_send()


def attend(parent, lengths, table, qn, qr, ku, vu, pool, recent, nl):
    any_spec = pl.BlockSpec(memory_space=pl.ANY)
    smem = pl.BlockSpec(memory_space=pltpu.SMEM)
    dma = pltpu.SemaphoreType.DMA
    return pl.pallas_call(
        attend_kernel,
        out_shape=jax.ShapeDtypeStruct((ROWS, HEADS * VDIM), BF),
        in_specs=[smem] * 3 + [any_spec] * 7,
        out_specs=pl.BlockSpec(memory_space=pltpu.VMEM),
        scratch_shapes=[
            pltpu.VMEM((ROWS, HEADS * NOPE), BF),
            pltpu.VMEM((QROWS, ROPE), BF),
            pltpu.VMEM((HEADS, NOPE, LAT), BF),
            pltpu.VMEM((HEADS, LAT, VDIM), BF),
            pltpu.VMEM((B_DEV, WIDTH, BLOCK), BF),
            pltpu.VMEM((ROWS, WIDTH), BF),
            pltpu.VMEM((WIDTH, 128), BF),
            pltpu.VMEM((LANES, QROWS, 128), F32),
            pltpu.VMEM((LANES, QROWS, 128), F32),
            pltpu.VMEM((QROWS, 128), F32),
            pltpu.VMEM((QROWS, 128), F32),
            pltpu.VMEM((B_DEV, PART, 128), BF),
            pltpu.VMEM((GROUPS, PART, 128), BF),
            pltpu.VMEM((GROUPS, PART, 128), BF),
            pltpu.VMEM((1, 128), jnp.int32),
            pltpu.VMEM((GROUPS, 1, 128), jnp.int32),
            pltpu.VMEM((GROUPS, 1, 128), jnp.int32),
            pltpu.SMEM((GROUPS, 1, 128), jnp.int32),
            pltpu.VMEM((8, PAIRS, PART, 128), BF),
            pltpu.VMEM((PAIRS, WIDTH, BLOCK), BF),
            dma((7,)), dma,
            dma((GROUPS,)), dma((GROUPS,)), dma((GROUPS,)), dma((GROUPS,)),
            dma((4,)), dma((4,)), dma((5,)), dma((5,)),
        ],
        compiler_params=pltpu.CompilerParams(
            collective_id=0, has_side_effects=True, vmem_limit_bytes=48 * 2**20
        ),
        cost_estimate=pl.CostEstimate(flops=1_300_000_000, bytes_accessed=12_000_000, transcendentals=400_000),
    )(parent, lengths, table, qn, qr, ku, vu, pool, recent, nl)


def project(att, wt):
    vmem = pl.BlockSpec(memory_space=pltpu.VMEM)
    dma = pltpu.SemaphoreType.DMA
    return pl.pallas_call(
        project_kernel,
        out_shape=jax.ShapeDtypeStruct((NX * ROWS, COLS), BF),
        in_specs=[vmem, vmem],
        out_specs=vmem,
        scratch_shapes=[
            pltpu.VMEM((8, ROWS, HEADS * VDIM), BF),
            pltpu.VMEM((8, ROWS, NX * COLS), BF),
            pltpu.VMEM((8, ROWS, NX * COLS), BF),
            pltpu.VMEM((NX, ROWS, COLS), BF),
            pltpu.VMEM((NX, ROWS, COLS), BF),
            dma((2, 4, 2)), dma((2, 4, 2)), dma((8,)), dma((8,)), dma((NX,)), dma((NX,)),
        ],
        compiler_params=pltpu.CompilerParams(
            collective_id=1, has_side_effects=True, vmem_limit_bytes=48 * 2**20
        ),
        cost_estimate=pl.CostEstimate(flops=2_900_000_000, bytes_accessed=6_000_000, transcendentals=0),
    )(att, wt)


def local(
    query_nope, query_rope, key_up, value_up, out_weight, block_pool, recent_blocks, new_latent,
    parent, lengths, block_table,
):
    groups = [[zz * NX + xx for xx in range(NX)] for zz in range(NZ)]
    wt = lax.all_gather(out_weight.T, "branch", axis=0, tiled=True, axis_index_groups=groups)
    att = attend(
        parent, lengths, block_table.reshape(B_DEV), query_nope, query_rope.reshape(QROWS, ROPE), key_up, value_up,
        jnp.swapaxes(block_pool, 1, 2), jnp.swapaxes(recent_blocks, 1, 2), new_latent,
    )
    return project(att, wt)


def solution(mesh):
    return jax.shard_map(
        local,
        mesh=mesh,
        in_specs=(
            P("branch", "head"),
            P("branch", "head"),
            P("head", None, None),
            P("head", None, None),
            P("head", "branch"),
            P("branch", None, None),
            P("branch", None, None),
            P("branch", None),
            P("branch"),
            P("branch"),
            P("branch", None),
        ),
        out_specs=P("head", "branch"),
        check_vma=False,
    )
```

```python
import functools

import jax
import jax.numpy as jnp
from jax import lax
from jax.experimental import pallas as pl
from jax.experimental.pallas import tpu as pltpu
from jax.sharding import PartitionSpec as P

NOPE = 128
ROPE = 64
LAT = 512
VDIM = 128
BLOCK = 128
STEPS = 4
B_DEV = 24
PAIRS = B_DEV // 2
WIDTH = LAT + ROPE
HEADS = 16
ROWS = B_DEV * STEPS
HALF = ROWS // 2
QROWS = ROWS * HEADS
COLS = 224
NZ, NX, NY = 8, 4, 4
GROUPS = NZ * NX
PART = 80
VMEM_BYTES = 60 * 2**20
LANES = LAT // 128
SCALE = (NOPE + ROPE) ** -0.5
BF = jnp.bfloat16
F32 = jnp.float32
MESH = pl.DeviceIdType.MESH
NT = (((1,), (1,)), ((), ()))


def dot(a, b):
    return jnp.dot(a, b, preferred_element_type=F32)


def dot_nt(a, b):
    return lax.dot_general(a, b, NT, preferred_element_type=F32)


def remote(src, dst, send, recv, **where):
    return pltpu.make_async_remote_copy(
        src_ref=src, dst_ref=dst, send_sem=send, recv_sem=recv,
        device_id=where, device_id_type=MESH,
    )


def layer_kernel(
    par_hbm, lens_hbm, table_hbm,
    qn_hbm, qr_hbm, ku_hbm, vu_hbm, pool_hbm, recent_hbm, nl_hbm, w_hbm,
    out,
    par, lens, table,
    qn, qr, ku, vu, pool, nl, nlt, wt,
    qs, ctx, peak, total,
    mine, packed, slots, my_par, all_par, pick_v, pick_s, parts, fork,
    held, made, landed, cut, final,
    load_sem, pick_sem, par_send, par_recv, out_send, out_recv, ring_send, ring_recv, core_send, core_recv,
    w_send, w_recv, z_send, z_recv, r_send, r_recv, x_send, x_recv,
):
    me = lax.axis_index("branch")
    head = lax.axis_index("head")
    z, x = me // NX, lax.rem(me, NX)
    y, core = head // 2, lax.rem(head, 2)
    up, down = lax.rem(y + 1, NY), lax.rem(y + 3, NY)
    far = lax.rem(y + 2, NY)
    left, right = lax.rem(x + 3, NX), lax.rem(x + 1, NX)
    nxt = lax.rem(z + 1, NZ) * NX + x
    prv = lax.rem(z + NZ - 1, NZ) * NX + x
    row0 = pl.multiple_of(y * 144 + core * 64, 16)

    def columns(i, start=0, size=COLS):
        return wt.at[pl.ds(pl.multiple_of(i * COLS + start, 16), size)]

    pairs = (
        (par_hbm, par), (recent_hbm.at[:, pl.ds(row0, PART), :], mine), (ku_hbm, ku), (qn_hbm, qn), (qr_hbm, qr),
        (lens_hbm, lens), (table_hbm, table), (pool_hbm, pool), (nl_hbm, nl), (vu_hbm, vu), (w_hbm, columns(x)),
    )
    loads = [pltpu.make_async_copy(src, dst, load_sem.at[i]) for i, (src, dst) in enumerate(pairs)]
    for load in loads:
        load.start()

    barrier = pltpu.get_barrier_semaphore()

    def greet(i, _):
        pl.semaphore_signal(barrier, inc=1, device_id={"branch": lax.rem(me + i, GROUPS)}, device_id_type=MESH)
        return 0

    lax.fori_loop(1, GROUPS, greet, 0)
    for i in range(1, 8):
        pl.semaphore_signal(barrier, inc=1, device_id={"head": lax.rem(head + i, 8)}, device_id_type=MESH)

    loads[0].wait()
    lane = lax.broadcasted_iota(jnp.int32, (1, 128), 1)
    row = jnp.zeros((1, 128), jnp.int32) - 1
    for b in range(0, B_DEV, 2):
        row = jnp.where(lane == b, par[b], row)
    my_par[...] = row
    all_par[me] = row
    pl.semaphore_wait(barrier, GROUPS - 1 + 7)

    def start_par(i, _):
        d = lax.rem(me + i, GROUPS)
        remote(my_par, all_par.at[me], par_send.at[i], par_recv.at[me], branch=d).start()
        return 0

    lax.fori_loop(1, GROUPS, start_par, 0)

    loads[2].wait()
    loads[3].wait()
    for h in range(HEADS):
        q = dot(qn[:, h * NOPE:(h + 1) * NOPE], ku[h]).astype(BF).astype(F32)
        for j in range(LANES):
            qs[j, pl.ds(h, ROWS, stride=HEADS), :] = q[:, j * 128:(j + 1) * 128]
    loads[4].wait()
    low = lax.broadcasted_iota(jnp.int32, (ROWS, 128), 1) < ROPE
    for h in range(HEADS):
        q = qr[:, (h // 2) * 128:(h // 2 + 1) * 128].astype(F32)
        qs[LANES, pl.ds(h, ROWS, stride=HEADS), :] = jnp.where(low if h % 2 == 0 else ~low, q, 0.0)

    def wait_par(i, _):
        src = lax.rem(me + i, GROUPS)
        remote(my_par, all_par.at[src], par_send.at[i], par_recv.at[src], branch=src).wait()
        return 0

    lax.fori_loop(1, GROUPS, wait_par, 0)
    local = all_par[...] - me * B_DEV
    hit = (local >= 0) & (local < B_DEV)
    pick_v[...] = jnp.broadcast_to(
        jnp.sum(jnp.where(hit, local, 0), axis=2, keepdims=True), (GROUPS, 1, 128)
    )
    pick = pltpu.make_async_copy(pick_v, pick_s, pick_sem)
    pick.start()
    loads[1].wait()
    pick.wait()

    def send_block(i, _):
        d = lax.rem(me + i, GROUPS)
        packed[d] = mine[pick_s[d, 0, 0]]
        remote(packed.at[d], slots.at[me], out_send.at[d], out_recv.at[me], branch=d).start()
        return 0

    lax.fori_loop(1, GROUPS, send_block, 0)
    slots[me] = mine[pick_s[me, 0, 0]]

    loads[10].wait()

    def share(n, owner, start, size, to):
        return remote(
            columns(owner, start, size), columns(owner, start, size), w_send.at[n], w_recv.at[n], branch=z * NX + to
        )

    share(0, x, 0, COLS, right).start()
    share(1, x, 0, COLS, left).start()

    for n in (5, 6, 7, 8):
        loads[n].wait()
    nlt[...] = jnp.zeros_like(nlt)
    nlt[:, :ROWS] = nl[...].astype(F32).T.astype(BF)

    key = lax.broadcasted_iota(jnp.int32, (STEPS * HEADS, 256), 1)
    step = lax.broadcasted_iota(jnp.int32, (STEPS * HEADS, 256), 0) // HEADS

    def query(rows):
        return jnp.concatenate([qs[j, rows, :] for j in range(LANES + 1)], axis=1).astype(BF)

    def scores(rows, keys):
        return dot(query(rows), jnp.concatenate([keys, keys[LAT:]], axis=0))

    def prefix(b, _):
        rows = pl.ds(pl.multiple_of(b * 64, 64), 64)
        keys = jnp.concatenate([pool[table[b]], nlt[...]], axis=1)
        s = scores(rows, keys)
        fresh = key - BLOCK - b * STEPS
        allowed = (key < lens[b]) | ((fresh >= 0) & (fresh <= step))
        s = jnp.where(allowed, s * SCALE, -jnp.inf)
        m = jnp.max(s, axis=1, keepdims=True)
        w = jnp.exp(s - m).astype(BF)
        total[rows, :] = jnp.broadcast_to(jnp.sum(w.astype(F32), axis=1, keepdims=True), (64, 128))
        peak[rows, :] = jnp.broadcast_to(m, (64, 128))
        c = dot_nt(w, keys[:LAT])
        for j in range(LANES):
            ctx[j, rows, :] = c[:, j * 128:(j + 1) * 128]
        return 0

    lax.fori_loop(0, B_DEV // 2, prefix, 0)

    def wait_block(i, _):
        src = lax.rem(me + i, GROUPS)
        remote(packed.at[src], slots.at[src], out_send.at[src], out_recv.at[src], branch=src).wait()
        return 0

    lax.fori_loop(1, GROUPS, wait_block, 0)
    for p in range(PAIRS):
        parts[head, p] = slots[par[2 * p] // B_DEV]

    def piece(h, half):
        at = parts.at[h]
        return at if half is None else at.at[pl.ds(half * (PAIRS // 2), PAIRS // 2)]

    def ring(n, h, half, to):
        return remote(piece(h, half), piece(h, half), ring_send.at[n], ring_recv.at[n], head=to * 2 + core)

    def swap(n, h, half):
        return remote(piece(h, half), piece(h, half), core_send.at[n], core_recv.at[n], head=y * 2 + 1 - core)

    ring(0, head, None, up).start()
    ring(1, head, None, down).start()
    swap(0, head, None).start()

    lax.fori_loop(B_DEV // 2, B_DEV * 3 // 4, prefix, 0)

    from_down, from_up, from_far = down * 2 + core, up * 2 + core, far * 2 + core
    ring(0, from_down, None, up).wait()
    ring(2, from_down, 0, up).start()
    swap(1, from_down, None).start()
    ring(1, from_up, None, down).wait()
    ring(3, from_up, 1, down).start()
    swap(2, from_up, None).start()

    lax.fori_loop(B_DEV * 3 // 4, B_DEV, prefix, 0)

    share(0, left, 0, COLS, right).wait()
    share(2, left, 0, COLS // 2, right).start()
    share(1, right, 0, COLS, left).wait()
    share(3, right, COLS // 2, COLS // 2, left).start()

    ring(2, from_far, 0, up).wait()
    swap(3, from_far, 0).start()
    ring(3, from_far, 1, down).wait()
    swap(4, from_far, 1).start()
    other = 1 - core
    swap(0, y * 2 + other, None).wait()
    swap(1, down * 2 + other, None).wait()
    swap(2, up * 2 + other, None).wait()
    swap(3, far * 2 + other, 0).wait()
    swap(4, far * 2 + other, 1).wait()

    def gather(p, _):
        for yy in range(NY):
            fork[p, yy * 144:yy * 144 + 80] = parts[2 * yy, p]
            fork[p, yy * 144 + 80:yy * 144 + 144] = parts[2 * yy + 1, p, 16:80]
        return 0

    lax.fori_loop(0, PAIRS, gather, 0)

    def forked(p, _):
        rows = pl.ds(pl.multiple_of(p * 128, 128), 128)
        keys = fork[p]
        s = scores(rows, keys) * SCALE
        old = peak[rows, :][:, :1]
        m = jnp.maximum(jnp.max(s, axis=1, keepdims=True), old)
        w = jnp.exp(s - m).astype(BF)
        back = jnp.exp(old - m)
        norm = total[rows, :][:, :1] * back + jnp.sum(w.astype(F32), axis=1, keepdims=True)
        c = dot_nt(w, keys[:LAT])
        scale = 1.0 / norm
        for j in range(LANES):
            both = (ctx[j, rows, :] * back + c[:, j * 128:(j + 1) * 128]) * scale
            ctx[j, rows, :] = both.astype(BF).astype(F32)
        return 0

    def half_of(slot, s):
        return held.at[slot, pl.ds(s * HALF, HALF)]

    def hop(way, k, s):
        came, goes = (k - 1, k) if way == 0 else ((9 - k) % 8, 8 - k)
        return remote(
            half_of(came, s), half_of(goes, s), z_send.at[way, k - 1, s], z_recv.at[way, k - 1, s],
            branch=nxt if way == 0 else prv,
        )

    hops = []

    def go(way, k, s):
        c = hop(way, k, s)
        c.start()
        hops.append(c)

    loads[9].wait()
    for s in (0, 1):
        lax.fori_loop(s * (PAIRS // 2), (s + 1) * (PAIRS // 2), forked, 0)
        for h in range(HEADS):
            c = [ctx[j, pl.ds(s * HALF * HEADS + h, HALF, stride=HEADS), :] for j in range(LANES)]
            c = jnp.concatenate(c, axis=1).astype(BF)
            held[0, s * HALF:(s + 1) * HALF, h * VDIM:(h + 1) * VDIM] = dot(c, vu[h]).astype(BF)
        go(0, 1, s)
        go(1, 1, s)

    share(2, lax.rem(x + 2, NX), 0, COLS // 2, right).wait()
    share(3, lax.rem(x + 2, NX), COLS // 2, COLS // 2, left).wait()

    def reduce_copy(slot):
        return remote(made.at[slot], landed.at[head], r_send.at[slot], r_recv.at[head], head=lax.rem(z + 8 - slot, 8))

    def multiply(slot):
        made[slot] = dot_nt(held[slot], wt[...]).astype(BF)

        @pl.when(lax.rem(z + 8 - slot, 8) != head)
        def _():
            reduce_copy(slot).start()

    multiply(0)
    for k in (1, 2, 3):
        for s in (0, 1):
            for way in (0, 1):
                t = s if way == 0 else 1 - s
                hop(way, k, t).wait_recv()
                if k < 3 or t == way:
                    go(way, k + 1, t)
            if s == 0 and k > 1:
                multiply(9 - k)
        multiply(k)
    multiply(5)
    hop(0, 4, 0).wait_recv()
    hop(1, 4, 1).wait_recv()
    multiply(4)

    acc = made[lax.rem(z + 8 - head, 8)].astype(F32)
    for i in range(1, 8):
        src = lax.rem(head + i, 8)
        remote(made.at[0], landed.at[src], r_send.at[0], r_recv.at[src], head=src).wait_recv()
        acc = acc + landed[src].astype(F32)
    acc = acc.astype(BF)
    for i in range(NX):
        cut[i] = acc[:, i * COLS:(i + 1) * COLS]
    final[x] = cut[x]
    spread = []
    for i in range(1, NX):
        d = lax.rem(x + i, NX)
        c = remote(cut.at[d], final.at[x], x_send.at[i], x_recv.at[x], branch=z * NX + d)
        c.start()
        spread.append(c)
    for i in range(1, NX):
        d = lax.rem(x + i, NX)
        remote(cut.at[d], final.at[d], x_send.at[i], x_recv.at[d], branch=z * NX + d).wait_recv()
    for i in range(NX):
        out[i * ROWS:(i + 1) * ROWS, :] = final[i]

    for c in hops:
        c.wait_send()
    for c in spread:
        c.wait_send()
    for slot in range(8):

        @pl.when(lax.rem(z + 8 - slot, 8) != head)
        def _(slot=slot):
            reduce_copy(slot).wait_send()


def layer(*operands):
    vmem, dma = pltpu.VMEM, pltpu.SemaphoreType.DMA
    smem = pltpu.SMEM
    return pl.pallas_call(
        layer_kernel,
        out_shape=jax.ShapeDtypeStruct((NX * ROWS, COLS), BF),
        in_specs=[pl.BlockSpec(memory_space=pl.ANY)] * 11,
        out_specs=pl.BlockSpec(memory_space=pltpu.VMEM),
        scratch_shapes=[
            smem((B_DEV,), jnp.int32), smem((B_DEV,), jnp.int32), smem((B_DEV,), jnp.int32),
            vmem((ROWS, HEADS * NOPE), BF),
            vmem((ROWS, HEADS * ROPE), BF),
            vmem((HEADS, NOPE, LAT), BF),
            vmem((HEADS, LAT, VDIM), BF),
            vmem((B_DEV, WIDTH, BLOCK), BF),
            vmem((ROWS, WIDTH), BF),
            vmem((WIDTH, 128), BF),
            vmem((NX * COLS, HEADS * VDIM), BF),
            vmem((LANES + 1, QROWS, 128), F32),
            vmem((LANES, QROWS, 128), F32),
            vmem((QROWS, 128), F32),
            vmem((QROWS, 128), F32),
            vmem((B_DEV, PART, 128), BF),
            vmem((GROUPS, PART, 128), BF),
            vmem((GROUPS, PART, 128), BF),
            vmem((1, 128), jnp.int32),
            vmem((GROUPS, 1, 128), jnp.int32),
            vmem((GROUPS, 1, 128), jnp.int32),
            smem((GROUPS, 1, 128), jnp.int32),
            vmem((8, PAIRS, PART, 128), BF),
            vmem((PAIRS, WIDTH, BLOCK), BF),
            vmem((8, ROWS, HEADS * VDIM), BF),
            vmem((8, ROWS, NX * COLS), BF),
            vmem((8, ROWS, NX * COLS), BF),
            vmem((NX, ROWS, COLS), BF),
            vmem((NX, ROWS, COLS), BF),
            dma((11,)), dma,
            dma((GROUPS,)), dma((GROUPS,)), dma((GROUPS,)), dma((GROUPS,)),
            dma((4,)), dma((4,)), dma((5,)), dma((5,)),
            dma((4,)), dma((4,)), dma((2, 4, 2)), dma((2, 4, 2)), dma((8,)), dma((8,)), dma((NX,)), dma((NX,)),
        ],
        compiler_params=pltpu.CompilerParams(
            collective_id=0, has_side_effects=True, vmem_limit_bytes=VMEM_BYTES
        ),
        cost_estimate=pl.CostEstimate(flops=4_200_000_000, bytes_accessed=16_000_000, transcendentals=400_000),
    )(*operands)


def local(
    query_nope, query_rope, key_up, value_up, out_weight, block_pool, recent_blocks, new_latent,
    parent, lengths, block_table,
):
    return layer(
        parent, lengths, block_table.reshape(B_DEV), query_nope, query_rope, key_up, value_up,
        jnp.swapaxes(block_pool, 1, 2), jnp.swapaxes(recent_blocks, 1, 2), new_latent, out_weight.T,
    )


def solution(mesh):
    return jax.shard_map(
        local,
        mesh=mesh,
        in_specs=(
            P("branch", "head"),
            P("branch", "head"),
            P("head", None, None),
            P("head", None, None),
            P("head", "branch"),
            P("branch", None, None),
            P("branch", None, None),
            P("branch", None),
            P("branch"),
            P("branch"),
            P("branch", None),
        ),
        out_specs=P("head", "branch"),
        check_vma=False,
    )
```

```python
import functools

import jax
import jax.numpy as jnp
from jax import lax
from jax.experimental import pallas as pl
from jax.experimental.pallas import tpu as pltpu
from jax.sharding import PartitionSpec as P

NOPE = 128
ROPE = 64
LAT = 512
VDIM = 128
BLOCK = 128
STEPS = 4
B_DEV = 24
PAIRS = B_DEV // 2
WIDTH = LAT + ROPE
HEADS = 16
ROWS = B_DEV * STEPS
HALF = ROWS // 2
QROWS = ROWS * HEADS
COLS = 224
NZ, NX, NY = 8, 4, 4
GROUPS = NZ * NX
PART_A, PART_B = 48, 32
PART = PART_A + PART_B
SLICE = COLS // 2
VMEM_BYTES = 60 * 2**20
LANES = LAT // 128
TOGETHER = 3
LAG = 2
SCALE = (NOPE + ROPE) ** -0.5
BF = jnp.bfloat16
F32 = jnp.float32
MESH = pl.DeviceIdType.MESH
NT = (((1,), (1,)), ((), ()))


SIZES = (32, 16)


def dot(a, b):
    return jnp.dot(a, b, preferred_element_type=F32)


def dot_nt(a, b):
    return lax.dot_general(a, b, NT, preferred_element_type=F32)


def remote(src, dst, send, recv, **where):
    return pltpu.make_async_remote_copy(
        src_ref=src, dst_ref=dst, send_sem=send, recv_sem=recv,
        device_id=where, device_id_type=MESH,
    )


def layer_kernel(
    par_hbm, lens_hbm, table_hbm,
    qn_hbm, qr_hbm, ku_hbm, vu_hbm, pool_hbm, recent_hbm, nl_hbm, w_hbm,
    out,
    par, lens, table,
    qn, qr, ku, vu, pool, nl, nlt, wt,
    qs, ctx, peak, total,
    mine, packed, slots_a, slots_b, my_par, all_par, pick_v, pick_s, parts_a, parts_b,
    held, made, landed, done, final,
    load_sem, pick_sem, par_send, par_recv, out_send, out_recv, ring_send, ring_recv, core_send, core_recv,
    w_send, w_recv, z_send, z_recv, r_send, r_recv, f_send, f_recv,
):
    me = lax.axis_index("branch")
    head = lax.axis_index("head")
    z, x = me // NX, lax.rem(me, NX)
    y, core = head // 2, lax.rem(head, 2)
    up, down = lax.rem(y + 1, NY), lax.rem(y + 3, NY)
    far = lax.rem(y + 2, NY)
    left, right = lax.rem(x + 3, NX), lax.rem(x + 1, NX)
    nxt = lax.rem(z + 1, NZ) * NX + x
    prv = lax.rem(z + NZ - 1, NZ) * NX + x
    row0 = pl.multiple_of(y * 144 + core * PART, 16)

    def columns(i, start=0, size=COLS):
        return wt.at[pl.ds(pl.multiple_of(i * COLS + start, 16), size)]

    pairs = (
        (par_hbm, par), (recent_hbm.at[:, pl.ds(row0, 64), :], mine.at[:, pl.ds(0, 64), :]), (ku_hbm, ku), (qn_hbm, qn), (qr_hbm, qr),
        (lens_hbm, lens), (table_hbm, table), (pool_hbm, pool), (nl_hbm, nl), (vu_hbm, vu), (w_hbm, columns(x)),
    )
    loads = [pltpu.make_async_copy(src, dst, load_sem.at[i]) for i, (src, dst) in enumerate(pairs)]
    for load in loads:
        load.start()

    def extra():
        return pltpu.make_async_copy(
            recent_hbm.at[:, pl.ds(pl.multiple_of(y * 144 + 64, 16), 16), :], mine.at[:, pl.ds(64, 16), :], load_sem.at[11]
        )

    @pl.when(core == 0)
    def _():
        extra().start()

    @pl.when(core == 1)
    def _():
        mine[:, 64:, :] = jnp.zeros((B_DEV, 16, 128), BF)

    barrier = pltpu.get_barrier_semaphore()

    def greet(i, _):
        pl.semaphore_signal(barrier, inc=1, device_id={"branch": lax.rem(me + i, GROUPS)}, device_id_type=MESH)
        return 0

    lax.fori_loop(1, GROUPS, greet, 0)
    for i in range(1, 8):
        pl.semaphore_signal(barrier, inc=1, device_id={"head": lax.rem(head + i, 8)}, device_id_type=MESH)
    for i in range(NX):
        for n in range(2):

            @pl.when((i != x) | (2 * x + n != head))
            def _(i=i, n=n):
                pl.semaphore_signal(
                    barrier, inc=1, device_id={"branch": z * NX + i, "head": 2 * x + n}, device_id_type=MESH
                )

    loads[0].wait()
    lane = lax.broadcasted_iota(jnp.int32, (1, 128), 1)
    row = jnp.zeros((1, 128), jnp.int32) - 1
    for b in range(0, B_DEV, 2):
        row = jnp.where(lane == b, par[b], row)
    my_par[...] = row
    all_par[me] = row
    pl.semaphore_wait(barrier, GROUPS - 1 + 7 + jnp.where(y == x, 7, 8))

    def start_par(i, _):
        d = lax.rem(me + i, GROUPS)
        remote(my_par, all_par.at[me], par_send.at[i], par_recv.at[me], branch=d).start()
        return 0

    lax.fori_loop(1, GROUPS, start_par, 0)

    loads[2].wait()
    loads[3].wait()
    for h in range(HEADS):
        q = dot(qn[:, h * NOPE:(h + 1) * NOPE], ku[h]).astype(BF).astype(F32)
        for j in range(LANES):
            qs[j, pl.ds(h, ROWS, stride=HEADS), :] = q[:, j * 128:(j + 1) * 128]
    loads[4].wait()
    low = lax.broadcasted_iota(jnp.int32, (ROWS, 128), 1) < ROPE
    for h in range(HEADS):
        q = qr[:, (h // 2) * 128:(h // 2 + 1) * 128].astype(F32)
        qs[LANES, pl.ds(h, ROWS, stride=HEADS), :] = jnp.where(low if h % 2 == 0 else ~low, q, 0.0)

    def wait_par(i, _):
        src = lax.rem(me + i, GROUPS)
        remote(my_par, all_par.at[src], par_send.at[i], par_recv.at[src], branch=src).wait()
        return 0

    lax.fori_loop(1, GROUPS, wait_par, 0)
    local = all_par[...] - me * B_DEV
    hit = (local >= 0) & (local < B_DEV)
    pick_v[...] = jnp.broadcast_to(
        jnp.sum(jnp.where(hit, local, 0), axis=2, keepdims=True), (GROUPS, 1, 128)
    )
    pick = pltpu.make_async_copy(pick_v, pick_s, pick_sem)
    pick.start()
    loads[1].wait()

    @pl.when(core == 0)
    def _():
        extra().wait()

    pick.wait()

    def block_a(n, at, to):
        return remote(packed.at[n, pl.ds(0, PART_A)], slots_a.at[at], out_send.at[0, n], out_recv.at[0, at], branch=to)

    def block_b(n, at, to, size):
        return remote(
            packed.at[n, pl.ds(PART_A, size)], slots_b.at[at, pl.ds(0, size)],
            out_send.at[1, n], out_recv.at[1, at], branch=to,
        )

    def send_a(i, _):
        d = lax.rem(me + i, GROUPS)
        packed[d] = mine[pick_s[d, 0, 0]]
        block_a(d, me, d).start()
        return 0

    lax.fori_loop(1, GROUPS, send_a, 0)

    for c in range(2):

        @pl.when(core == c)
        def _(c=c):
            def send_b(i, _):
                d = lax.rem(me + i, GROUPS)
                block_b(d, me, d, SIZES[c]).start()
                return 0

            lax.fori_loop(1, GROUPS, send_b, 0)

    own = mine[pick_s[me, 0, 0]]
    slots_a[me] = own[:PART_A]
    slots_b[me] = own[PART_A:]

    loads[10].wait()

    def share(n, owner, start, size, to):
        return remote(
            columns(owner, start, size), columns(owner, start, size), w_send.at[n], w_recv.at[n], branch=z * NX + to
        )

    share(0, x, 0, COLS, right).start()
    share(1, x, 0, COLS, left).start()

    for n in (5, 6, 7, 8):
        loads[n].wait()
    nlt[...] = jnp.zeros_like(nlt)
    nlt[:, :ROWS] = nl[...].astype(F32).T.astype(BF)

    key = lax.broadcasted_iota(jnp.int32, (STEPS * HEADS, 256), 1)
    step = lax.broadcasted_iota(jnp.int32, (STEPS * HEADS, 256), 0) // HEADS

    def query(rows):
        return jnp.concatenate([qs[j, rows, :] for j in range(LANES + 1)], axis=1).astype(BF)

    def scores(rows, keys):
        return dot(query(rows), jnp.concatenate([keys, keys[LAT:]], axis=0))

    def prefix(b, _):
        rows = pl.ds(pl.multiple_of(b * 64, 64), 64)
        keys = jnp.concatenate([pool[table[b]], nlt[...]], axis=1)
        s = scores(rows, keys)
        fresh = key - BLOCK - b * STEPS
        allowed = (key < lens[b]) | ((fresh >= 0) & (fresh <= step))
        s = jnp.where(allowed, s * SCALE, -jnp.inf)
        m = jnp.max(s, axis=1, keepdims=True)
        w = jnp.exp(s - m).astype(BF)
        total[rows, :] = jnp.broadcast_to(jnp.sum(w.astype(F32), axis=1, keepdims=True), (64, 128))
        peak[rows, :] = jnp.broadcast_to(m, (64, 128))
        c = dot_nt(w, keys[:LAT])
        for j in range(LANES):
            ctx[j, rows, :] = c[:, j * 128:(j + 1) * 128]
        return 0

    lax.fori_loop(0, B_DEV // 2, prefix, 0)

    def wait_a(i, _):
        src = lax.rem(me + i, GROUPS)
        block_a(src, src, src).wait()
        return 0

    lax.fori_loop(1, GROUPS, wait_a, 0)
    for p in range(PAIRS):
        parts_a[head, p] = slots_a[par[2 * p] // B_DEV]

    from_down, from_up, from_far = down * 2 + core, up * 2 + core, far * 2 + core
    other = 1 - core

    def piece(h, part, size, half):
        at = parts_a.at[h] if part == 0 else parts_b.at[h, :, pl.ds(0, size)]
        return at if half is None else at.at[pl.ds(half * (PAIRS // 2), PAIRS // 2)]

    def ring(n, h, part, size, half, to):
        at = piece(h, part, size, half)
        return remote(at, at, ring_send.at[part, n], ring_recv.at[part, n], head=to * 2 + core)

    def swap(n, h, part, size, half):
        at = piece(h, part, size, half)
        return remote(at, at, core_send.at[part, n], core_recv.at[part, n], head=y * 2 + other)

    def ring_first(part, size):
        ring(0, head, part, size, None, up).start()
        ring(1, head, part, size, None, down).start()
        swap(0, head, part, size, None).start()

    def ring_second(part, size):
        ring(0, from_down, part, size, None, up).wait()
        ring(2, from_down, part, size, 0, up).start()
        ring(1, from_up, part, size, None, down).wait()
        ring(3, from_up, part, size, 1, down).start()
        swap(1, from_down, part, size, None).start()
        swap(2, from_up, part, size, None).start()

    def ring_third(part, size):
        ring(2, from_far, part, size, 0, up).wait()
        swap(3, from_far, part, size, 0).start()
        ring(3, from_far, part, size, 1, down).wait()
        swap(4, from_far, part, size, 1).start()

    def ring_end(part, size, other_size):
        for n, h, half in ((0, head, None), (1, from_down, None), (2, from_up, None), (3, from_far, 0), (4, from_far, 1)):
            swap(n, h, part, size, half).wait_send()
            swap(n, h + other - core, part, other_size, half).wait_recv()

    ring_first(0, PART_A)
    lax.fori_loop(B_DEV // 2, B_DEV * 3 // 4, prefix, 0)
    ring_second(0, PART_A)
    lax.fori_loop(B_DEV * 3 // 4, B_DEV, prefix, 0)
    ring_third(0, PART_A)

    for c in range(2):

        @pl.when(core == c)
        def _(c=c):
            def wait_b(i, _):
                src = lax.rem(me + i, GROUPS)
                block_b(src, src, src, SIZES[c]).wait()
                return 0

            lax.fori_loop(1, GROUPS, wait_b, 0)
            for p in range(PAIRS):
                parts_b[head, p] = slots_b[par[2 * p] // B_DEV]
            ring_first(1, SIZES[c])

    share(0, left, 0, COLS, right).wait()
    share(2, left, 0, COLS // 2, right).start()
    share(1, right, 0, COLS, left).wait()
    share(3, right, COLS // 2, COLS // 2, left).start()

    for c in range(2):

        @pl.when(core == c)
        def _(c=c):
            ring_second(1, SIZES[c])
            ring_third(1, SIZES[c])
            ring_end(1, SIZES[c], SIZES[1 - c])

    ring_end(0, PART_A, PART_A)

    def forked(n, _):
        several = range(TOGETHER)
        rows = [pl.ds(pl.multiple_of((n * TOGETHER + i) * 128, 128), 128) for i in several]
        keys = []
        for i in several:
            p = n * TOGETHER + i
            found = []
            for yy in range(NY):
                found += [parts_a[2 * yy, p], parts_b[2 * yy, p], parts_a[2 * yy + 1, p], parts_b[2 * yy + 1, p, :SIZES[1]]]
            keys.append(jnp.concatenate(found, axis=0))
        s = [scores(rows[i], keys[i]) * SCALE for i in several]
        old = [peak[rows[i], :][:, :1] for i in several]
        m = [jnp.maximum(jnp.max(s[i], axis=1, keepdims=True), old[i]) for i in several]
        w = [jnp.exp(s[i] - m[i]).astype(BF) for i in several]
        back = [jnp.exp(old[i] - m[i]) for i in several]
        norm = [
            total[rows[i], :][:, :1] * back[i] + jnp.sum(w[i].astype(F32), axis=1, keepdims=True) for i in several
        ]
        c = [dot_nt(w[i], keys[i][:LAT]) for i in several]
        scale = [1.0 / norm[i] for i in several]
        both = [
            [(ctx[j, rows[i], :] * back[i] + c[i][:, j * 128:(j + 1) * 128]) * scale[i] for j in range(LANES)]
            for i in several
        ]
        for i in several:
            for j in range(LANES):
                ctx[j, rows[i], :] = both[i][j].astype(BF).astype(F32)
        return 0

    def half_of(slot, s):
        return held.at[slot, pl.ds(s * HALF, HALF)]

    def hop(way, k, s):
        came, goes = (k - 1, k) if way == 0 else ((9 - k) % 8, 8 - k)
        return remote(
            half_of(came, s), half_of(goes, s), z_send.at[way, k - 1, s], z_recv.at[way, k - 1, s],
            branch=nxt if way == 0 else prv,
        )

    hops = []

    def go(way, k, s):
        c = hop(way, k, s)
        c.start()
        hops.append(c)

    loads[9].wait()
    for s in (0, 1):
        lax.fori_loop(s * (PAIRS // 2) // TOGETHER, (s + 1) * (PAIRS // 2) // TOGETHER, forked, 0)
        for h in range(HEADS):
            c = [ctx[j, pl.ds(s * HALF * HEADS + h, HALF, stride=HEADS), :] for j in range(LANES)]
            c = jnp.concatenate(c, axis=1).astype(BF)
            held[0, s * HALF:(s + 1) * HALF, h * VDIM:(h + 1) * VDIM] = dot(c, vu[h]).astype(BF)
        go(0, 1, s)
        go(1, 1, s)

    share(2, lax.rem(x + 2, NX), 0, COLS // 2, right).wait()
    share(3, lax.rem(x + 2, NX), COLS // 2, COLS // 2, left).wait()

    def reduce_copy(slot, to):
        return remote(made.at[slot, to], landed.at[slot, head], r_send.at[slot, to], r_recv.at[slot, head], head=to)

    def multiply(slot):
        for g in range(NX):
            r = dot_nt(held[slot], wt[g * COLS:(g + 1) * COLS]).astype(BF)
            for n in range(2):
                to = 2 * g + n
                made[slot, to] = r[:, n * SLICE:(n + 1) * SLICE]

                @pl.when(to != head)
                def _(to=to):
                    reduce_copy(slot, to).start()

    def is_mine(slot):
        return (y == x) & (lax.rem(z + 8 - slot, 8) == head)

    def final_copy(slot):
        return remote(
            done.at[slot], final.at[x, core], f_send.at[slot], f_recv.at[x, core],
            branch=z * NX + y, head=lax.rem(z + 8 - slot, 8),
        )

    def fold(slot):
        acc = made[slot, head].astype(F32)
        for i in range(1, 8):
            src = lax.rem(head + i, 8)
            remote(
                made.at[slot, src], landed.at[slot, src], r_send.at[slot, src], r_recv.at[slot, src], head=src
            ).wait_recv()
            acc = acc + landed[slot, src].astype(F32)
        done[slot] = acc.astype(BF)
        mine_too = is_mine(slot)

        @pl.when(mine_too)
        def _():
            final[x, core] = done[slot]

        @pl.when(~mine_too)
        def _():
            final_copy(slot).start()

    waiting = []

    def turn(slot):
        multiply(slot)
        waiting.append(slot)
        if len(waiting) > LAG:
            fold(waiting.pop(0))

    turn(0)
    for k in (1, 2, 3):
        for s in (0, 1):
            for way in (0, 1):
                t = s if way == 0 else 1 - s
                hop(way, k, t).wait_recv()
                if k < 3 or t == way:
                    go(way, k + 1, t)
            if s == 0 and k > 1:
                turn(9 - k)
        turn(k)
    turn(5)
    hop(0, 4, 0).wait_recv()
    hop(1, 4, 1).wait_recv()
    turn(4)
    for slot in waiting:
        fold(slot)

    for i in range(NX):
        for n in range(2):

            @pl.when((i != x) | (2 * x + n != head))
            def _(i=i, n=n):
                remote(
                    done.at[0], final.at[i, n], f_send.at[0], f_recv.at[i, n], branch=z * NX + i, head=2 * x + n
                ).wait_recv()

        out[i * ROWS:(i + 1) * ROWS, :] = jnp.concatenate([final[i, 0], final[i, 1]], axis=1)

    for c in hops:
        c.wait_send()
    for slot in range(8):

        @pl.when(~is_mine(slot))
        def _(slot=slot):
            final_copy(slot).wait_send()

        def sent(i, _, slot=slot):
            reduce_copy(slot, lax.rem(head + i, 8)).wait_send()
            return 0

        lax.fori_loop(1, 8, sent, 0)


def layer(*operands):
    vmem, dma = pltpu.VMEM, pltpu.SemaphoreType.DMA
    smem = pltpu.SMEM
    return pl.pallas_call(
        layer_kernel,
        out_shape=jax.ShapeDtypeStruct((NX * ROWS, COLS), BF),
        in_specs=[pl.BlockSpec(memory_space=pl.ANY)] * 11,
        out_specs=pl.BlockSpec(memory_space=pltpu.VMEM),
        scratch_shapes=[
            smem((B_DEV,), jnp.int32), smem((B_DEV,), jnp.int32), smem((B_DEV,), jnp.int32),
            vmem((ROWS, HEADS * NOPE), BF),
            vmem((ROWS, HEADS * ROPE), BF),
            vmem((HEADS, NOPE, LAT), BF),
            vmem((HEADS, LAT, VDIM), BF),
            vmem((B_DEV, WIDTH, BLOCK), BF),
            vmem((ROWS, WIDTH), BF),
            vmem((WIDTH, 128), BF),
            vmem((NX * COLS, HEADS * VDIM), BF),
            vmem((LANES + 1, QROWS, 128), F32),
            vmem((LANES, QROWS, 128), F32),
            vmem((QROWS, 128), F32),
            vmem((QROWS, 128), F32),
            vmem((B_DEV, PART, 128), BF),
            vmem((GROUPS, PART, 128), BF),
            vmem((GROUPS, PART_A, 128), BF),
            vmem((GROUPS, PART_B, 128), BF),
            vmem((1, 128), jnp.int32),
            vmem((GROUPS, 1, 128), jnp.int32),
            vmem((GROUPS, 1, 128), jnp.int32),
            smem((GROUPS, 1, 128), jnp.int32),
            vmem((8, PAIRS, PART_A, 128), BF),
            vmem((8, PAIRS, PART_B, 128), BF),
            vmem((8, ROWS, HEADS * VDIM), BF),
            vmem((8, 8, ROWS, SLICE), BF),
            vmem((8, 8, ROWS, SLICE), BF),
            vmem((8, ROWS, SLICE), BF),
            vmem((NX, 2, ROWS, SLICE), BF),
            dma((12,)), dma,
            dma((GROUPS,)), dma((GROUPS,)), dma((2, GROUPS)), dma((2, GROUPS)),
            dma((2, 4)), dma((2, 4)), dma((2, 5)), dma((2, 5)),
            dma((4,)), dma((4,)), dma((2, 4, 2)), dma((2, 4, 2)), dma((8, 8)), dma((8, 8)), dma((8,)), dma((NX, 2)),
        ],
        compiler_params=pltpu.CompilerParams(
            collective_id=0, has_side_effects=True, vmem_limit_bytes=VMEM_BYTES
        ),
        cost_estimate=pl.CostEstimate(flops=4_200_000_000, bytes_accessed=16_000_000, transcendentals=400_000),
    )(*operands)


def local(
    query_nope, query_rope, key_up, value_up, out_weight, block_pool, recent_blocks, new_latent,
    parent, lengths, block_table,
):
    return layer(
        parent, lengths, block_table.reshape(B_DEV), query_nope, query_rope, key_up, value_up,
        jnp.swapaxes(block_pool, 1, 2), jnp.swapaxes(recent_blocks, 1, 2), new_latent, out_weight.T,
    )


def solution(mesh):
    return jax.shard_map(
        local,
        mesh=mesh,
        in_specs=(
            P("branch", "head"),
            P("branch", "head"),
            P("head", None, None),
            P("head", None, None),
            P("head", "branch"),
            P("branch", None, None),
            P("branch", None, None),
            P("branch", None),
            P("branch"),
            P("branch"),
            P("branch", None),
        ),
        out_specs=P("head", "branch"),
        check_vma=False,
    )
```

```python
import functools

import jax
import jax.numpy as jnp
from jax import lax
from jax.experimental import pallas as pl
from jax.experimental.pallas import tpu as pltpu
from jax.sharding import PartitionSpec as P

NOPE = 128
ROPE = 64
LAT = 512
VDIM = 128
BLOCK = 128
STEPS = 4
B_DEV = 24
PAIRS = B_DEV // 2
WIDTH = LAT + ROPE
HEADS = 16
ROWS = B_DEV * STEPS
HALF = ROWS // 2
QROWS = ROWS * HEADS
COLS = 224
NZ, NX, NY = 8, 4, 4
GROUPS = NZ * NX
PART = 80
CHUNK = PAIRS // 2
SLICE = COLS // 2
VMEM_BYTES = 60 * 2**20
LANES = LAT // 128
TOGETHER = 1
SCALE = (NOPE + ROPE) ** -0.5
BF = jnp.bfloat16
F32 = jnp.float32
MESH = pl.DeviceIdType.MESH
NT = (((1,), (1,)), ((), ()))


SIZES = (80, 64)
ORDER = (0, 3, 1, 2)


def dot(a, b):
    return jnp.dot(a, b, preferred_element_type=F32)


def dot_nt(a, b):
    return lax.dot_general(a, b, NT, preferred_element_type=F32)


def remote(src, dst, send, recv, **where):
    return pltpu.make_async_remote_copy(
        src_ref=src, dst_ref=dst, send_sem=send, recv_sem=recv,
        device_id=where, device_id_type=MESH,
    )


def layer_kernel(
    par_hbm, lens_hbm, table_hbm,
    qn_hbm, qr_hbm, ku_hbm, vu_hbm, pool_hbm, recent_hbm, nl_hbm, w_hbm,
    out,
    par, lens, table,
    qn, qr, ku, vu, pool, nl, nlt, wt,
    qs, ctx, peak, total,
    mine, packed, slots, my_par, all_par, pick_v, pick_s, parts, fork,
    held, made, met, summed, done, final,
    load_sem, pick_sem, par_send, par_recv, out_send, out_recv, ring_send, ring_recv, core_send, core_recv,
    w_send, w_recv, z_send, z_recv, r_send, r_recv, f_send, f_recv,
):
    me = lax.axis_index("branch")
    head = lax.axis_index("head")
    z, x = me // NX, lax.rem(me, NX)
    y, core = head // 2, lax.rem(head, 2)
    up, down = lax.rem(y + 1, NY), lax.rem(y + 3, NY)
    far = lax.rem(y + 2, NY)
    left, right = lax.rem(x + 3, NX), lax.rem(x + 1, NX)
    nxt = lax.rem(z + 1, NZ) * NX + x
    prv = lax.rem(z + NZ - 1, NZ) * NX + x
    row0 = pl.multiple_of(y * 144 + core * PART, 16)

    def columns(i, start=0, size=COLS):
        return wt.at[pl.ds(pl.multiple_of(i * COLS + start, 16), size)]

    pairs = (
        (par_hbm, par), (recent_hbm.at[:, pl.ds(row0, 64), :], mine.at[:, pl.ds(0, 64), :]), (ku_hbm, ku), (qn_hbm, qn), (qr_hbm, qr),
        (lens_hbm, lens), (table_hbm, table), (pool_hbm, pool), (nl_hbm, nl), (vu_hbm, vu), (w_hbm, columns(x)),
    )
    loads = [pltpu.make_async_copy(src, dst, load_sem.at[i]) for i, (src, dst) in enumerate(pairs)]
    for load in loads:
        load.start()

    def extra():
        return pltpu.make_async_copy(
            recent_hbm.at[:, pl.ds(pl.multiple_of(y * 144 + 64, 16), 16), :], mine.at[:, pl.ds(64, 16), :], load_sem.at[11]
        )

    @pl.when(core == 0)
    def _():
        extra().start()

    @pl.when(core == 1)
    def _():
        mine[:, 64:, :] = jnp.zeros((B_DEV, 16, 128), BF)

    barrier = pltpu.get_barrier_semaphore()

    def greet(i, _):
        pl.semaphore_signal(barrier, inc=1, device_id={"branch": lax.rem(me + i, GROUPS)}, device_id_type=MESH)
        return 0

    lax.fori_loop(1, GROUPS, greet, 0)
    for i in range(1, 8):
        pl.semaphore_signal(barrier, inc=1, device_id={"head": lax.rem(head + i, 8)}, device_id_type=MESH)
    for i in range(NX):
        for n in range(2):

            @pl.when((i != x) | (2 * x + n != head))
            def _(i=i, n=n):
                pl.semaphore_signal(
                    barrier, inc=1, device_id={"branch": z * NX + i, "head": 2 * x + n}, device_id_type=MESH
                )

    loads[0].wait()
    lane = lax.broadcasted_iota(jnp.int32, (1, 128), 1)
    row = jnp.zeros((1, 128), jnp.int32) - 1
    for b in range(0, B_DEV, 2):
        row = jnp.where(lane == b, par[b], row)
    my_par[...] = row
    all_par[me] = row
    pl.semaphore_wait(barrier, GROUPS - 1 + 7 + jnp.where(y == x, 7, 8))

    def start_par(i, _):
        d = lax.rem(me + i, GROUPS)
        remote(my_par, all_par.at[me], par_send.at[i], par_recv.at[me], branch=d).start()
        return 0

    lax.fori_loop(1, GROUPS, start_par, 0)

    loads[2].wait()
    loads[3].wait()
    for h in range(HEADS):
        q = dot(qn[:, h * NOPE:(h + 1) * NOPE], ku[h]).astype(BF).astype(F32)
        for j in range(LANES):
            qs[j, pl.ds(h, ROWS, stride=HEADS), :] = q[:, j * 128:(j + 1) * 128]
    loads[4].wait()
    low = lax.broadcasted_iota(jnp.int32, (ROWS, 128), 1) < ROPE
    for h in range(HEADS):
        q = qr[:, (h // 2) * 128:(h // 2 + 1) * 128].astype(F32)
        qs[LANES, pl.ds(h, ROWS, stride=HEADS), :] = jnp.where(low if h % 2 == 0 else ~low, q, 0.0)

    def wait_par(i, _):
        src = lax.rem(me + i, GROUPS)
        remote(my_par, all_par.at[src], par_send.at[i], par_recv.at[src], branch=src).wait()
        return 0

    lax.fori_loop(1, GROUPS, wait_par, 0)
    local = all_par[...] - me * B_DEV
    hit = (local >= 0) & (local < B_DEV)
    pick_v[...] = jnp.broadcast_to(
        jnp.sum(jnp.where(hit, local, 0), axis=2, keepdims=True), (GROUPS, 1, 128)
    )
    pick = pltpu.make_async_copy(pick_v, pick_s, pick_sem)
    pick.start()
    loads[1].wait()

    @pl.when(core == 0)
    def _():
        extra().wait()

    pick.wait()

    def block(n, at, to, size):
        return remote(
            packed.at[n, pl.ds(0, size)], slots.at[at, pl.ds(0, size)], out_send.at[n], out_recv.at[at], branch=to
        )

    for c in range(2):

        @pl.when(core == c)
        def _(c=c):
            def send_block(i, _):
                d = lax.rem(me + i, GROUPS)
                packed[d] = mine[pick_s[d, 0, 0]]
                block(d, me, d, SIZES[c]).start()
                return 0

            lax.fori_loop(1, GROUPS, send_block, 0)

    slots[me] = mine[pick_s[me, 0, 0]]

    loads[10].wait()

    def share(n, owner, start, size, to):
        return remote(
            columns(owner, start, size), columns(owner, start, size), w_send.at[n], w_recv.at[n], branch=z * NX + to
        )

    share(0, x, 0, COLS, right).start()
    share(1, x, 0, COLS, left).start()

    for n in (5, 6, 7, 8):
        loads[n].wait()
    nlt[...] = jnp.zeros_like(nlt)
    nlt[:, :ROWS] = nl[...].astype(F32).T.astype(BF)

    key = lax.broadcasted_iota(jnp.int32, (STEPS * HEADS, 256), 1)
    step = lax.broadcasted_iota(jnp.int32, (STEPS * HEADS, 256), 0) // HEADS

    def query(rows):
        return jnp.concatenate([qs[j, rows, :] for j in range(LANES + 1)], axis=1).astype(BF)

    def scores(rows, keys):
        return dot(query(rows), jnp.concatenate([keys, keys[LAT:]], axis=0))

    def prefix(b, _):
        rows = pl.ds(pl.multiple_of(b * 64, 64), 64)
        keys = jnp.concatenate([pool[table[b]], nlt[...]], axis=1)
        s = scores(rows, keys)
        fresh = key - BLOCK - b * STEPS
        allowed = (key < lens[b]) | ((fresh >= 0) & (fresh <= step))
        s = jnp.where(allowed, s * SCALE, -jnp.inf)
        m = jnp.max(s, axis=1, keepdims=True)
        w = jnp.exp(s - m).astype(BF)
        total[rows, :] = jnp.broadcast_to(jnp.sum(w.astype(F32), axis=1, keepdims=True), (64, 128))
        peak[rows, :] = jnp.broadcast_to(m, (64, 128))
        c = dot_nt(w, keys[:LAT])
        for j in range(LANES):
            ctx[j, rows, :] = c[:, j * 128:(j + 1) * 128]
        return 0

    lax.fori_loop(0, B_DEV // 2, prefix, 0)

    from_down, from_up, from_far = down * 2 + core, up * 2 + core, far * 2 + core
    other = 1 - core

    def piece(h, ch, size, half):
        first, count = (ch * CHUNK, CHUNK) if half is None else (ch * CHUNK + half * (CHUNK // 2), CHUNK // 2)
        return parts.at[h, pl.ds(first, count), pl.ds(0, size)]

    def ring(n, h, ch, size, half, to):
        at = piece(h, ch, size, half)
        return remote(at, at, ring_send.at[ch, n], ring_recv.at[ch, n], head=to * 2 + core)

    def swap(n, h, ch, size, half):
        at = piece(h, ch, size, half)
        return remote(at, at, core_send.at[ch, n], core_recv.at[ch, n], head=y * 2 + other)

    def ring_first(ch, size):
        ring(0, head, ch, size, None, up).start()
        ring(1, head, ch, size, None, down).start()
        swap(0, head, ch, size, None).start()

    def ring_second(ch, size):
        ring(0, from_down, ch, size, None, up).wait()
        ring(2, from_down, ch, size, 0, up).start()
        ring(1, from_up, ch, size, None, down).wait()
        ring(3, from_up, ch, size, 1, down).start()
        swap(1, from_down, ch, size, None).start()
        swap(2, from_up, ch, size, None).start()

    def ring_third(ch, size):
        ring(2, from_far, ch, size, 0, up).wait()
        swap(3, from_far, ch, size, 0).start()
        ring(3, from_far, ch, size, 1, down).wait()
        swap(4, from_far, ch, size, 1).start()

    def ring_end(ch, size, other_size):
        for n, h, half in ((0, head, None), (1, from_down, None), (2, from_up, None), (3, from_far, 0), (4, from_far, 1)):
            swap(n, h, ch, size, half).wait_send()
            swap(n, h + other - core, ch, other_size, half).wait_recv()

    for c in range(2):

        @pl.when(core == c)
        def _(c=c):
            def wait_block(i, _):
                src = lax.rem(me + i, GROUPS)
                block(src, src, src, SIZES[c]).wait()
                return 0

            lax.fori_loop(1, GROUPS, wait_block, 0)
            for ch in range(2):
                for p in range(ch * CHUNK, (ch + 1) * CHUNK):
                    parts[head, p] = slots[par[2 * p] // B_DEV]
                ring_first(ch, SIZES[c])

    lax.fori_loop(B_DEV // 2, B_DEV, prefix, 0)

    for c in range(2):

        @pl.when(core == c)
        def _(c=c):
            ring_second(0, SIZES[c])
            ring_second(1, SIZES[c])
            ring_third(0, SIZES[c])
            ring_third(1, SIZES[c])

    share(0, left, 0, COLS, right).wait()
    share(2, left, 0, COLS // 2, right).start()
    share(1, right, 0, COLS, left).wait()
    share(3, right, COLS // 2, COLS // 2, left).start()

    def arrive(ch):
        for c in range(2):

            @pl.when(core == c)
            def _(c=c):
                ring_end(ch, SIZES[c], SIZES[1 - c])

        def gather(p, _):
            for yy in range(NY):
                fork[p, yy * 144:yy * 144 + 80] = parts[2 * yy, p]
                fork[p, yy * 144 + 80:yy * 144 + 144] = parts[2 * yy + 1, p, :64]
            return 0

        lax.fori_loop(ch * CHUNK, (ch + 1) * CHUNK, gather, 0)

    def forked(n, _):
        several = range(TOGETHER)
        rows = [pl.ds(pl.multiple_of((n * TOGETHER + i) * 128, 128), 128) for i in several]
        keys = [fork[n * TOGETHER + i] for i in several]
        s = [scores(rows[i], keys[i]) * SCALE for i in several]
        old = [peak[rows[i], :][:, :1] for i in several]
        m = [jnp.maximum(jnp.max(s[i], axis=1, keepdims=True), old[i]) for i in several]
        w = [jnp.exp(s[i] - m[i]).astype(BF) for i in several]
        back = [jnp.exp(old[i] - m[i]) for i in several]
        norm = [
            total[rows[i], :][:, :1] * back[i] + jnp.sum(w[i].astype(F32), axis=1, keepdims=True) for i in several
        ]
        c = [dot_nt(w[i], keys[i][:LAT]) for i in several]
        scale = [1.0 / norm[i] for i in several]
        both = [
            [(ctx[j, rows[i], :] * back[i] + c[i][:, j * 128:(j + 1) * 128]) * scale[i] for j in range(LANES)]
            for i in several
        ]
        for i in several:
            for j in range(LANES):
                ctx[j, rows[i], :] = both[i][j].astype(BF).astype(F32)
        return 0

    def half_of(slot, s):
        return held.at[slot, pl.ds(s * HALF, HALF)]

    def hop(way, k, s):
        came, goes = (k - 1, k) if way == 0 else ((9 - k) % 8, 8 - k)
        return remote(
            half_of(came, s), half_of(goes, s), z_send.at[way, k - 1, s], z_recv.at[way, k - 1, s],
            branch=nxt if way == 0 else prv,
        )

    hops = []

    def go(way, k, s):
        c = hop(way, k, s)
        c.start()
        hops.append(c)

    loads[9].wait()
    for s in (0, 1):
        arrive(s)
        lax.fori_loop(s * (PAIRS // 2) // TOGETHER, (s + 1) * (PAIRS // 2) // TOGETHER, forked, 0)
        for h in range(HEADS):
            c = [ctx[j, pl.ds(s * HALF * HEADS + h, HALF, stride=HEADS), :] for j in range(LANES)]
            c = jnp.concatenate(c, axis=1).astype(BF)
            held[0, s * HALF:(s + 1) * HALF, h * VDIM:(h + 1) * VDIM] = dot(c, vu[h]).astype(BF)
        go(0, 1, s)
        go(1, 1, s)

    share(2, lax.rem(x + 2, NX), 0, COLS // 2, right).wait()
    share(3, lax.rem(x + 2, NX), COLS // 2, COLS // 2, left).wait()

    group = jnp.where((y == 0) | (y == 3), 0, 1)
    near = jnp.where(lax.rem(y, 2) == 0, y + 1, y - 1)
    upper = y // 2

    def halve(n, slot):
        if n == 0:
            return remote(
                made.at[slot, other], met.at[slot, pl.ds(0, 4)], r_send.at[0, slot], r_recv.at[0, slot], head=y * 2 + other
            )
        if n == 1:
            return remote(
                summed.at[slot, pl.ds(2 * (1 - group), 2)], met.at[slot, pl.ds(4, 2)],
                r_send.at[1, slot], r_recv.at[1, slot], head=near * 2 + core,
            )
        return remote(
            summed.at[slot, 4 + 1 - upper], met.at[slot, 6], r_send.at[2, slot], r_recv.at[2, slot], head=(3 - y) * 2 + core
        )

    def multiply(slot):
        for i, g in enumerate(ORDER):
            r = dot_nt(held[slot], wt[g * COLS:(g + 1) * COLS]).astype(BF)
            for n in range(2):
                made[slot, n, i] = r[:, n * SLICE:(n + 1) * SLICE]
        halve(0, slot).start()

    def fold_core(slot):
        halve(0, slot).wait_recv()
        for i in range(4):
            summed[slot, i] = (made[slot, core, i].astype(F32) + met[slot, i].astype(F32)).astype(BF)
        halve(1, slot).start()

    def fold_near(slot):
        halve(1, slot).wait_recv()
        for i in range(2):
            summed[slot, 4 + i] = (summed[slot, 2 * group + i].astype(F32) + met[slot, 4 + i].astype(F32)).astype(BF)
        halve(2, slot).start()

    def is_mine(slot):
        return (y == x) & (lax.rem(z + 8 - slot, 8) == head)

    def final_copy(slot):
        return remote(
            done.at[slot], final.at[x, core], f_send.at[slot], f_recv.at[x, core],
            branch=z * NX + y, head=lax.rem(z + 8 - slot, 8),
        )

    def fold(slot):
        halve(2, slot).wait_recv()
        done[slot] = (summed[slot, 4 + upper].astype(F32) + met[slot, 6].astype(F32)).astype(BF)
        mine_too = is_mine(slot)

        @pl.when(mine_too)
        def _():
            final[x, core] = done[slot]

        @pl.when(~mine_too)
        def _():
            final_copy(slot).start()

    order = (0, 1, 7, 2, 6, 3, 5, 4)

    def turn(slot):
        n = order.index(slot)
        multiply(slot)
        for lag, step in ((1, fold_core), (2, fold_near), (3, fold)):
            if n >= lag:
                step(order[n - lag])

    turn(0)
    for k in (1, 2, 3):
        for s in (0, 1):
            for way in (0, 1):
                t = s if way == 0 else 1 - s
                hop(way, k, t).wait_recv()
                if k < 3 or t == way:
                    go(way, k + 1, t)
            if s == 0 and k > 1:
                turn(9 - k)
        turn(k)
    turn(5)
    hop(0, 4, 0).wait_recv()
    hop(1, 4, 1).wait_recv()
    turn(4)
    fold_core(4)
    fold_near(5)
    fold(3)
    fold_near(4)
    fold(5)
    fold(4)

    for i in range(NX):
        for n in range(2):

            @pl.when((i != x) | (2 * x + n != head))
            def _(i=i, n=n):
                remote(
                    done.at[0], final.at[i, n], f_send.at[0], f_recv.at[i, n], branch=z * NX + i, head=2 * x + n
                ).wait_recv()

        out[i * ROWS:(i + 1) * ROWS, :] = jnp.concatenate([final[i, 0], final[i, 1]], axis=1)

    for c in hops:
        c.wait_send()
    for slot in range(8):

        @pl.when(~is_mine(slot))
        def _(slot=slot):
            final_copy(slot).wait_send()

        for n in range(3):
            halve(n, slot).wait_send()


def layer(*operands):
    vmem, dma = pltpu.VMEM, pltpu.SemaphoreType.DMA
    smem = pltpu.SMEM
    return pl.pallas_call(
        layer_kernel,
        out_shape=jax.ShapeDtypeStruct((NX * ROWS, COLS), BF),
        in_specs=[pl.BlockSpec(memory_space=pl.ANY)] * 11,
        out_specs=pl.BlockSpec(memory_space=pltpu.VMEM),
        scratch_shapes=[
            smem((B_DEV,), jnp.int32), smem((B_DEV,), jnp.int32), smem((B_DEV,), jnp.int32),
            vmem((ROWS, HEADS * NOPE), BF),
            vmem((ROWS, HEADS * ROPE), BF),
            vmem((HEADS, NOPE, LAT), BF),
            vmem((HEADS, LAT, VDIM), BF),
            vmem((B_DEV, WIDTH, BLOCK), BF),
            vmem((ROWS, WIDTH), BF),
            vmem((WIDTH, 128), BF),
            vmem((NX * COLS, HEADS * VDIM), BF),
            vmem((LANES + 1, QROWS, 128), F32),
            vmem((LANES, QROWS, 128), F32),
            vmem((QROWS, 128), F32),
            vmem((QROWS, 128), F32),
            vmem((B_DEV, PART, 128), BF),
            vmem((GROUPS, PART, 128), BF),
            vmem((GROUPS, PART, 128), BF),
            vmem((1, 128), jnp.int32),
            vmem((GROUPS, 1, 128), jnp.int32),
            vmem((GROUPS, 1, 128), jnp.int32),
            smem((GROUPS, 1, 128), jnp.int32),
            vmem((8, PAIRS, PART, 128), BF),
            vmem((PAIRS, WIDTH, BLOCK), BF),
            vmem((8, ROWS, HEADS * VDIM), BF),
            vmem((8, 2, NY, ROWS, SLICE), BF),
            vmem((8, 7, ROWS, SLICE), BF),
            vmem((8, 6, ROWS, SLICE), BF),
            vmem((8, ROWS, SLICE), BF),
            vmem((NX, 2, ROWS, SLICE), BF),
            dma((12,)), dma,
            dma((GROUPS,)), dma((GROUPS,)), dma((GROUPS,)), dma((GROUPS,)),
            dma((2, 4)), dma((2, 4)), dma((2, 5)), dma((2, 5)),
            dma((4,)), dma((4,)), dma((2, 4, 2)), dma((2, 4, 2)), dma((3, 8)), dma((3, 8)), dma((8,)), dma((NX, 2)),
        ],
        compiler_params=pltpu.CompilerParams(
            collective_id=0, has_side_effects=True, vmem_limit_bytes=VMEM_BYTES
        ),
        cost_estimate=pl.CostEstimate(flops=4_200_000_000, bytes_accessed=16_000_000, transcendentals=400_000),
    )(*operands)


def local(
    query_nope, query_rope, key_up, value_up, out_weight, block_pool, recent_blocks, new_latent,
    parent, lengths, block_table,
):
    return layer(
        parent, lengths, block_table.reshape(B_DEV), query_nope, query_rope, key_up, value_up,
        jnp.swapaxes(block_pool, 1, 2), jnp.swapaxes(recent_blocks, 1, 2), new_latent, out_weight.T,
    )


def solution(mesh):
    return jax.shard_map(
        local,
        mesh=mesh,
        in_specs=(
            P("branch", "head"),
            P("branch", "head"),
            P("head", None, None),
            P("head", None, None),
            P("head", "branch"),
            P("branch", None, None),
            P("branch", None, None),
            P("branch", None),
            P("branch"),
            P("branch"),
            P("branch", None),
        ),
        out_specs=P("head", "branch"),
        check_vma=False,
    )
```

```python
import functools

import jax
import jax.numpy as jnp
from jax import lax
from jax.experimental import pallas as pl
from jax.experimental.pallas import tpu as pltpu
from jax.sharding import PartitionSpec as P

NOPE = 128
ROPE = 64
LAT = 512
VDIM = 128
BLOCK = 128
STEPS = 4
B_DEV = 24
PAIRS = B_DEV // 2
WIDTH = LAT + ROPE
HEADS = 16
ROWS = B_DEV * STEPS
HALF = ROWS // 2
QROWS = ROWS * HEADS
COLS = 224
NZ, NX, NY = 8, 4, 4
GROUPS = NZ * NX
PART = 80
CHUNK = PAIRS // 2
SLICE = COLS // 2
PADDED = 128
VMEM_BYTES = 60 * 2**20
LANES = LAT // 128
TOGETHER = 1
SCALE = (NOPE + ROPE) ** -0.5
BF = jnp.bfloat16
F32 = jnp.float32
MESH = pl.DeviceIdType.MESH
NT = (((1,), (1,)), ((), ()))


SIZES = (80, 64)
ORDER = (0, 3, 1, 2)


def dot(a, b):
    return jnp.dot(a, b, preferred_element_type=F32)


def dot_nt(a, b):
    return lax.dot_general(a, b, NT, preferred_element_type=F32)


def remote(src, dst, send, recv, **where):
    return pltpu.make_async_remote_copy(
        src_ref=src, dst_ref=dst, send_sem=send, recv_sem=recv,
        device_id=where, device_id_type=MESH,
    )


def layer_kernel(
    par_hbm, lens_hbm, table_hbm,
    qn_hbm, qr_hbm, ku_hbm, vu_hbm, pool_hbm, recent_hbm, nl_hbm, w_hbm,
    out,
    par, lens, table,
    qn, qr, ku, vu, pool, nl, nlt, wt,
    qs, ctx, peak, total,
    mine, packed, slots, my_par, all_par, pick_v, pick_s, parts, fork,
    held, made, met, summed, done, final,
    load_sem, pick_sem, par_send, par_recv, out_send, out_recv, ring_send, ring_recv, core_send, core_recv,
    w_send, w_recv, z_send, z_recv, r_send, r_recv, f_send, f_recv,
):
    me = lax.axis_index("branch")
    head = lax.axis_index("head")
    z, x = me // NX, lax.rem(me, NX)
    y, core = head // 2, lax.rem(head, 2)
    up, down = lax.rem(y + 1, NY), lax.rem(y + 3, NY)
    far = lax.rem(y + 2, NY)
    left, right = lax.rem(x + 3, NX), lax.rem(x + 1, NX)
    nxt = lax.rem(z + 1, NZ) * NX + x
    prv = lax.rem(z + NZ - 1, NZ) * NX + x
    row0 = pl.multiple_of(y * 144 + core * PART, 16)

    def columns(i, n):
        return wt.at[pl.ds(pl.multiple_of((2 * i + n) * PADDED, PADDED), SLICE)]

    pairs = (
        (par_hbm, par), (recent_hbm.at[:, pl.ds(row0, 64), :], mine.at[:, pl.ds(0, 64), :]), (ku_hbm, ku), (qn_hbm, qn), (qr_hbm, qr),
        (lens_hbm, lens), (table_hbm, table), (pool_hbm, pool), (nl_hbm, nl), (vu_hbm, vu), (w_hbm.at[pl.ds(0, SLICE)], columns(x, 0)),
        (w_hbm.at[pl.ds(SLICE, SLICE)], columns(x, 1)),
    )
    loads = [pltpu.make_async_copy(src, dst, load_sem.at[i]) for i, (src, dst) in enumerate(pairs)]
    for load in loads:
        load.start()

    def extra():
        return pltpu.make_async_copy(
            recent_hbm.at[:, pl.ds(pl.multiple_of(y * 144 + 64, 16), 16), :], mine.at[:, pl.ds(64, 16), :], load_sem.at[12]
        )

    @pl.when(core == 0)
    def _():
        extra().start()

    @pl.when(core == 1)
    def _():
        mine[:, 64:, :] = jnp.zeros((B_DEV, 16, 128), BF)

    barrier = pltpu.get_barrier_semaphore()

    def greet(i, _):
        pl.semaphore_signal(barrier, inc=1, device_id={"branch": lax.rem(me + i, GROUPS)}, device_id_type=MESH)
        return 0

    lax.fori_loop(1, GROUPS, greet, 0)
    for i in range(1, 8):
        pl.semaphore_signal(barrier, inc=1, device_id={"head": lax.rem(head + i, 8)}, device_id_type=MESH)
    for i in range(NX):
        for n in range(2):

            @pl.when((i != x) | (2 * x + n != head))
            def _(i=i, n=n):
                pl.semaphore_signal(
                    barrier, inc=1, device_id={"branch": z * NX + i, "head": 2 * x + n}, device_id_type=MESH
                )

    loads[0].wait()
    lane = lax.broadcasted_iota(jnp.int32, (1, 128), 1)
    row = jnp.zeros((1, 128), jnp.int32) - 1
    for b in range(0, B_DEV, 2):
        row = jnp.where(lane == b, par[b], row)
    my_par[...] = row
    all_par[me] = row
    pl.semaphore_wait(barrier, GROUPS - 1 + 7 + jnp.where(y == x, 7, 8))

    def start_par(i, _):
        d = lax.rem(me + i, GROUPS)
        remote(my_par, all_par.at[me], par_send.at[i], par_recv.at[me], branch=d).start()
        return 0

    lax.fori_loop(1, GROUPS, start_par, 0)

    loads[2].wait()
    loads[3].wait()
    for h in range(HEADS):
        q = dot(qn[:, h * NOPE:(h + 1) * NOPE], ku[h]).astype(BF).astype(F32)
        for j in range(LANES):
            qs[j, pl.ds(h, ROWS, stride=HEADS), :] = q[:, j * 128:(j + 1) * 128]
    loads[4].wait()
    low = lax.broadcasted_iota(jnp.int32, (ROWS, 128), 1) < ROPE
    for h in range(HEADS):
        q = qr[:, (h // 2) * 128:(h // 2 + 1) * 128].astype(F32)
        qs[LANES, pl.ds(h, ROWS, stride=HEADS), :] = jnp.where(low if h % 2 == 0 else ~low, q, 0.0)

    def wait_par(i, _):
        src = lax.rem(me + i, GROUPS)
        remote(my_par, all_par.at[src], par_send.at[i], par_recv.at[src], branch=src).wait()
        return 0

    lax.fori_loop(1, GROUPS, wait_par, 0)
    local = all_par[...] - me * B_DEV
    hit = (local >= 0) & (local < B_DEV)
    pick_v[...] = jnp.broadcast_to(
        jnp.sum(jnp.where(hit, local, 0), axis=2, keepdims=True), (GROUPS, 1, 128)
    )
    pick = pltpu.make_async_copy(pick_v, pick_s, pick_sem)
    pick.start()
    loads[1].wait()

    @pl.when(core == 0)
    def _():
        extra().wait()

    pick.wait()

    def block(n, at, to, size):
        return remote(
            packed.at[n, pl.ds(0, size)], slots.at[at, pl.ds(0, size)], out_send.at[n], out_recv.at[at], branch=to
        )

    for c in range(2):

        @pl.when(core == c)
        def _(c=c):
            def send_block(i, _):
                d = lax.rem(me + i, GROUPS)
                packed[d] = mine[pick_s[d, 0, 0]]
                block(d, me, d, SIZES[c]).start()
                return 0

            lax.fori_loop(1, GROUPS, send_block, 0)

    slots[me] = mine[pick_s[me, 0, 0]]

    for i in range(2 * NX):
        wt[i * PADDED + SLICE:(i + 1) * PADDED, :] = jnp.zeros((PADDED - SLICE, HEADS * VDIM), BF)
    loads[10].wait()
    loads[11].wait()

    def share(m, owner, n, to):
        return remote(columns(owner, n), columns(owner, n), w_send.at[m], w_recv.at[m], branch=z * NX + to)

    for n in range(2):
        share(n, x, n, right).start()
        share(2 + n, x, n, left).start()

    for n in (5, 6, 7, 8):
        loads[n].wait()
    nlt[...] = jnp.zeros_like(nlt)
    nlt[:, :ROWS] = nl[...].astype(F32).T.astype(BF)

    key = lax.broadcasted_iota(jnp.int32, (STEPS * HEADS, 256), 1)
    step = lax.broadcasted_iota(jnp.int32, (STEPS * HEADS, 256), 0) // HEADS

    def query(rows):
        return jnp.concatenate([qs[j, rows, :] for j in range(LANES + 1)], axis=1).astype(BF)

    def scores(rows, keys):
        return dot(query(rows), jnp.concatenate([keys, keys[LAT:]], axis=0))

    def prefix(b, _):
        rows = pl.ds(pl.multiple_of(b * 64, 64), 64)
        keys = jnp.concatenate([pool[table[b]], nlt[...]], axis=1)
        s = scores(rows, keys)
        fresh = key - BLOCK - b * STEPS
        allowed = (key < lens[b]) | ((fresh >= 0) & (fresh <= step))
        s = jnp.where(allowed, s * SCALE, -jnp.inf)
        m = jnp.max(s, axis=1, keepdims=True)
        w = jnp.exp(s - m).astype(BF)
        total[rows, :] = jnp.broadcast_to(jnp.sum(w.astype(F32), axis=1, keepdims=True), (64, 128))
        peak[rows, :] = jnp.broadcast_to(m, (64, 128))
        c = dot_nt(w, keys[:LAT])
        for j in range(LANES):
            ctx[j, rows, :] = c[:, j * 128:(j + 1) * 128]
        return 0

    lax.fori_loop(0, B_DEV // 2, prefix, 0)

    from_down, from_up, from_far = down * 2 + core, up * 2 + core, far * 2 + core
    other = 1 - core

    def piece(h, ch, size, half):
        first, count = (ch * CHUNK, CHUNK) if half is None else (ch * CHUNK + half * (CHUNK // 2), CHUNK // 2)
        return parts.at[h, pl.ds(first, count), pl.ds(0, size)]

    def ring(n, h, ch, size, half, to):
        at = piece(h, ch, size, half)
        return remote(at, at, ring_send.at[ch, n], ring_recv.at[ch, n], head=to * 2 + core)

    def swap(n, h, ch, size, half):
        at = piece(h, ch, size, half)
        return remote(at, at, core_send.at[ch, n], core_recv.at[ch, n], head=y * 2 + other)

    def ring_first(ch, size):
        ring(0, head, ch, size, None, up).start()
        ring(1, head, ch, size, None, down).start()
        swap(0, head, ch, size, None).start()

    def ring_second(ch, size):
        ring(0, from_down, ch, size, None, up).wait()
        ring(2, from_down, ch, size, 0, up).start()
        ring(1, from_up, ch, size, None, down).wait()
        ring(3, from_up, ch, size, 1, down).start()
        swap(1, from_down, ch, size, None).start()
        swap(2, from_up, ch, size, None).start()

    def ring_third(ch, size):
        ring(2, from_far, ch, size, 0, up).wait()
        swap(3, from_far, ch, size, 0).start()
        ring(3, from_far, ch, size, 1, down).wait()
        swap(4, from_far, ch, size, 1).start()

    def ring_end(ch, size, other_size):
        for n, h, half in ((0, head, None), (1, from_down, None), (2, from_up, None), (3, from_far, 0), (4, from_far, 1)):
            swap(n, h, ch, size, half).wait_send()
            swap(n, h + other - core, ch, other_size, half).wait_recv()

    for c in range(2):

        @pl.when(core == c)
        def _(c=c):
            def wait_block(i, _):
                src = lax.rem(me + i, GROUPS)
                block(src, src, src, SIZES[c]).wait()
                return 0

            lax.fori_loop(1, GROUPS, wait_block, 0)
            for ch in range(2):
                for p in range(ch * CHUNK, (ch + 1) * CHUNK):
                    parts[head, p] = slots[par[2 * p] // B_DEV]
                ring_first(ch, SIZES[c])

    lax.fori_loop(B_DEV // 2, B_DEV, prefix, 0)

    for c in range(2):

        @pl.when(core == c)
        def _(c=c):
            ring_second(0, SIZES[c])
            ring_second(1, SIZES[c])
            ring_third(0, SIZES[c])
            ring_third(1, SIZES[c])

    share(0, left, 0, right).wait()
    share(4, left, 0, right).start()
    share(3, right, 1, left).wait()
    share(5, right, 1, left).start()
    share(1, left, 1, right).wait()
    share(2, right, 0, left).wait()

    def arrive(ch):
        for c in range(2):

            @pl.when(core == c)
            def _(c=c):
                ring_end(ch, SIZES[c], SIZES[1 - c])

        def gather(p, _):
            for yy in range(NY):
                fork[p, yy * 144:yy * 144 + 80] = parts[2 * yy, p]
                fork[p, yy * 144 + 80:yy * 144 + 144] = parts[2 * yy + 1, p, :64]
            return 0

        lax.fori_loop(ch * CHUNK, (ch + 1) * CHUNK, gather, 0)

    def forked(n, _):
        several = range(TOGETHER)
        rows = [pl.ds(pl.multiple_of((n * TOGETHER + i) * 128, 128), 128) for i in several]
        keys = [fork[n * TOGETHER + i] for i in several]
        s = [scores(rows[i], keys[i]) * SCALE for i in several]
        old = [peak[rows[i], :][:, :1] for i in several]
        m = [jnp.maximum(jnp.max(s[i], axis=1, keepdims=True), old[i]) for i in several]
        w = [jnp.exp(s[i] - m[i]).astype(BF) for i in several]
        back = [jnp.exp(old[i] - m[i]) for i in several]
        norm = [
            total[rows[i], :][:, :1] * back[i] + jnp.sum(w[i].astype(F32), axis=1, keepdims=True) for i in several
        ]
        c = [dot_nt(w[i], keys[i][:LAT]) for i in several]
        scale = [1.0 / norm[i] for i in several]
        both = [
            [(ctx[j, rows[i], :] * back[i] + c[i][:, j * 128:(j + 1) * 128]) * scale[i] for j in range(LANES)]
            for i in several
        ]
        for i in several:
            for j in range(LANES):
                ctx[j, rows[i], :] = both[i][j].astype(BF).astype(F32)
        return 0

    def half_of(slot, s):
        return held.at[slot, pl.ds(s * HALF, HALF)]

    def hop(way, k, s):
        came, goes = (k - 1, k) if way == 0 else ((9 - k) % 8, 8 - k)
        return remote(
            half_of(came, s), half_of(goes, s), z_send.at[way, k - 1, s], z_recv.at[way, k - 1, s],
            branch=nxt if way == 0 else prv,
        )

    hops = []

    def go(way, k, s):
        c = hop(way, k, s)
        c.start()
        hops.append(c)

    loads[9].wait()
    for s in (0, 1):
        arrive(s)
        lax.fori_loop(s * (PAIRS // 2) // TOGETHER, (s + 1) * (PAIRS // 2) // TOGETHER, forked, 0)
        for h in range(HEADS):
            c = [ctx[j, pl.ds(s * HALF * HEADS + h, HALF, stride=HEADS), :] for j in range(LANES)]
            c = jnp.concatenate(c, axis=1).astype(BF)
            held[0, s * HALF:(s + 1) * HALF, h * VDIM:(h + 1) * VDIM] = dot(c, vu[h]).astype(BF)
        go(0, 1, s)
        go(1, 1, s)

    share(4, lax.rem(x + 2, NX), 0, right).wait()
    share(5, lax.rem(x + 2, NX), 1, left).wait()

    group = jnp.where((y == 0) | (y == 3), 0, 1)
    near = jnp.where(lax.rem(y, 2) == 0, y + 1, y - 1)
    upper = y // 2

    def halve(n, slot):
        if n == 0:
            return remote(
                made.at[slot, other], met.at[slot, pl.ds(0, 4)], r_send.at[0, slot], r_recv.at[0, slot], head=y * 2 + other
            )
        if n == 1:
            return remote(
                summed.at[slot, pl.ds(2 * (1 - group), 2)], met.at[slot, pl.ds(4, 2)],
                r_send.at[1, slot], r_recv.at[1, slot], head=near * 2 + core,
            )
        return remote(
            summed.at[slot, 4 + 1 - upper], met.at[slot, 6], r_send.at[2, slot], r_recv.at[2, slot], head=(3 - y) * 2 + core
        )

    def multiply(slot):
        for i, g in enumerate(ORDER):
            r = dot_nt(held[slot], wt[g * 2 * PADDED:(g + 1) * 2 * PADDED]).astype(BF)
            for n in range(2):
                made[slot, n, i] = r[:, n * PADDED:(n + 1) * PADDED]
        halve(0, slot).start()

    def fold_core(slot):
        halve(0, slot).wait_recv()
        for i in range(4):
            summed[slot, i] = (made[slot, core, i].astype(F32) + met[slot, i].astype(F32)).astype(BF)
        halve(1, slot).start()

    def fold_near(slot):
        halve(1, slot).wait_recv()
        for i in range(2):
            summed[slot, 4 + i] = (summed[slot, 2 * group + i].astype(F32) + met[slot, 4 + i].astype(F32)).astype(BF)
        halve(2, slot).start()

    def is_mine(slot):
        return (y == x) & (lax.rem(z + 8 - slot, 8) == head)

    def final_copy(slot):
        return remote(
            done.at[slot], final.at[x, core], f_send.at[slot], f_recv.at[x, core],
            branch=z * NX + y, head=lax.rem(z + 8 - slot, 8),
        )

    def fold(slot):
        halve(2, slot).wait_recv()
        done[slot] = (summed[slot, 4 + upper].astype(F32) + met[slot, 6].astype(F32)).astype(BF)
        mine_too = is_mine(slot)

        @pl.when(mine_too)
        def _():
            final[x, core] = done[slot]

        @pl.when(~mine_too)
        def _():
            final_copy(slot).start()

    order = (0, 1, 7, 2, 6, 3, 5, 4)

    def turn(slot):
        n = order.index(slot)
        multiply(slot)
        for lag, step in ((1, fold_core), (2, fold_near), (3, fold)):
            if n >= lag:
                step(order[n - lag])

    turn(0)
    for k in (1, 2, 3):
        for s in (0, 1):
            for way in (0, 1):
                t = s if way == 0 else 1 - s
                hop(way, k, t).wait_recv()
                if k < 3 or t == way:
                    go(way, k + 1, t)
            if s == 0 and k > 1:
                turn(9 - k)
        turn(k)
    turn(5)
    hop(0, 4, 0).wait_recv()
    hop(1, 4, 1).wait_recv()
    turn(4)
    fold_core(4)
    fold_near(5)
    fold(3)
    fold_near(4)
    fold(5)
    fold(4)

    for i in range(NX):
        for n in range(2):

            @pl.when((i != x) | (2 * x + n != head))
            def _(i=i, n=n):
                remote(
                    done.at[0], final.at[i, n], f_send.at[0], f_recv.at[i, n], branch=z * NX + i, head=2 * x + n
                ).wait_recv()

        out[i * ROWS:(i + 1) * ROWS, :] = jnp.concatenate([final[i, 0][:, :SLICE], final[i, 1][:, :SLICE]], axis=1)

    for c in hops:
        c.wait_send()
    for slot in range(8):

        @pl.when(~is_mine(slot))
        def _(slot=slot):
            final_copy(slot).wait_send()

        for n in range(3):
            halve(n, slot).wait_send()


def layer(*operands):
    vmem, dma = pltpu.VMEM, pltpu.SemaphoreType.DMA
    smem = pltpu.SMEM
    return pl.pallas_call(
        layer_kernel,
        out_shape=jax.ShapeDtypeStruct((NX * ROWS, COLS), BF),
        in_specs=[pl.BlockSpec(memory_space=pl.ANY)] * 11,
        out_specs=pl.BlockSpec(memory_space=pltpu.VMEM),
        scratch_shapes=[
            smem((B_DEV,), jnp.int32), smem((B_DEV,), jnp.int32), smem((B_DEV,), jnp.int32),
            vmem((ROWS, HEADS * NOPE), BF),
            vmem((ROWS, HEADS * ROPE), BF),
            vmem((HEADS, NOPE, LAT), BF),
            vmem((HEADS, LAT, VDIM), BF),
            vmem((B_DEV, WIDTH, BLOCK), BF),
            vmem((ROWS, WIDTH), BF),
            vmem((WIDTH, 128), BF),
            vmem((2 * NX * PADDED, HEADS * VDIM), BF),
            vmem((LANES + 1, QROWS, 128), F32),
            vmem((LANES, QROWS, 128), F32),
            vmem((QROWS, 128), F32),
            vmem((QROWS, 128), F32),
            vmem((B_DEV, PART, 128), BF),
            vmem((GROUPS, PART, 128), BF),
            vmem((GROUPS, PART, 128), BF),
            vmem((1, 128), jnp.int32),
            vmem((GROUPS, 1, 128), jnp.int32),
            vmem((GROUPS, 1, 128), jnp.int32),
            smem((GROUPS, 1, 128), jnp.int32),
            vmem((8, PAIRS, PART, 128), BF),
            vmem((PAIRS, WIDTH, BLOCK), BF),
            vmem((8, ROWS, HEADS * VDIM), BF),
            vmem((8, 2, NY, ROWS, PADDED), BF),
            vmem((8, 7, ROWS, PADDED), BF),
            vmem((8, 6, ROWS, PADDED), BF),
            vmem((8, ROWS, PADDED), BF),
            vmem((NX, 2, ROWS, PADDED), BF),
            dma((13,)), dma,
            dma((GROUPS,)), dma((GROUPS,)), dma((GROUPS,)), dma((GROUPS,)),
            dma((2, 4)), dma((2, 4)), dma((2, 5)), dma((2, 5)),
            dma((6,)), dma((6,)), dma((2, 4, 2)), dma((2, 4, 2)), dma((3, 8)), dma((3, 8)), dma((8,)), dma((NX, 2)),
        ],
        compiler_params=pltpu.CompilerParams(
            collective_id=0, has_side_effects=True, vmem_limit_bytes=VMEM_BYTES
        ),
        cost_estimate=pl.CostEstimate(flops=4_200_000_000, bytes_accessed=16_000_000, transcendentals=400_000),
    )(*operands)


def local(
    query_nope, query_rope, key_up, value_up, out_weight, block_pool, recent_blocks, new_latent,
    parent, lengths, block_table,
):
    return layer(
        parent, lengths, block_table.reshape(B_DEV), query_nope, query_rope, key_up, value_up,
        jnp.swapaxes(block_pool, 1, 2), jnp.swapaxes(recent_blocks, 1, 2), new_latent, out_weight.T,
    )


def solution(mesh):
    return jax.shard_map(
        local,
        mesh=mesh,
        in_specs=(
            P("branch", "head"),
            P("branch", "head"),
            P("head", None, None),
            P("head", None, None),
            P("head", "branch"),
            P("branch", None, None),
            P("branch", None, None),
            P("branch", None),
            P("branch"),
            P("branch"),
            P("branch", None),
        ),
        out_specs=P("head", "branch"),
        check_vma=False,
    )
```

```python
import functools

import jax
import jax.numpy as jnp
from jax import lax
from jax.experimental import pallas as pl
from jax.experimental.pallas import tpu as pltpu
from jax.sharding import PartitionSpec as P

NOPE = 128
ROPE = 64
LAT = 512
VDIM = 128
BLOCK = 128
STEPS = 4
B_DEV = 24
PAIRS = B_DEV // 2
WIDTH = LAT + ROPE
HEADS = 16
ROWS = B_DEV * STEPS
HALF = ROWS // 2
QROWS = ROWS * HEADS
COLS = 224
NZ, NX, NY = 8, 4, 4
GROUPS = NZ * NX
PART = 80
CHUNK = PAIRS // 2
SLICE = COLS // 2
PADDED = 128
VMEM_BYTES = 60 * 2**20
LANES = LAT // 128
TOGETHER = 1
SCALE = (NOPE + ROPE) ** -0.5
BF = jnp.bfloat16
F32 = jnp.float32
MESH = pl.DeviceIdType.MESH
NT = (((1,), (1,)), ((), ()))


SIZES = (80, 64)


def dot(a, b):
    return jnp.dot(a, b, preferred_element_type=F32)


def dot_nt(a, b):
    return lax.dot_general(a, b, NT, preferred_element_type=F32)


def remote(src, dst, send, recv, **where):
    return pltpu.make_async_remote_copy(
        src_ref=src, dst_ref=dst, send_sem=send, recv_sem=recv,
        device_id=where, device_id_type=MESH,
    )


def layer_kernel(
    par_hbm, lens_hbm, table_hbm,
    qn_hbm, qr_hbm, ku_hbm, vu_hbm, pool_hbm, recent_hbm, nl_hbm, w_hbm,
    out,
    par, lens, table,
    qn, qr, ku, vu, pool, nl, nlt, wt,
    qs, ctx, peak, total,
    mine, packed, slots, my_par, all_par, pick_v, pick_s, parts, fork,
    held, made, met, summed, landed,
    load_sem, pick_sem, par_send, par_recv, out_send, out_recv, ring_send, ring_recv, core_send, core_recv,
    w_send, w_recv, z_send, z_recv, r_send, r_recv, f_send, f_recv,
):
    me = lax.axis_index("branch")
    head = lax.axis_index("head")
    z, x = me // NX, lax.rem(me, NX)
    y, core = head // 2, lax.rem(head, 2)
    up, down = lax.rem(y + 1, NY), lax.rem(y + 3, NY)
    far = lax.rem(y + 2, NY)
    left, right = lax.rem(x + 3, NX), lax.rem(x + 1, NX)
    nxt = lax.rem(z + 1, NZ) * NX + x
    prv = lax.rem(z + NZ - 1, NZ) * NX + x
    row0 = pl.multiple_of(y * 144 + core * PART, 16)

    def columns(i, n):
        return wt.at[pl.ds(pl.multiple_of((2 * i + n) * PADDED, PADDED), SLICE)]

    pairs = (
        (par_hbm, par), (recent_hbm.at[:, pl.ds(row0, 64), :], mine.at[:, pl.ds(0, 64), :]), (ku_hbm, ku), (qn_hbm, qn), (qr_hbm, qr),
        (lens_hbm, lens), (table_hbm, table), (pool_hbm, pool), (nl_hbm, nl), (vu_hbm, vu), (w_hbm.at[pl.ds(0, SLICE)], columns(x, 0)),
        (w_hbm.at[pl.ds(SLICE, SLICE)], columns(x, 1)),
    )
    loads = [pltpu.make_async_copy(src, dst, load_sem.at[i]) for i, (src, dst) in enumerate(pairs)]
    for load in loads:
        load.start()

    def extra():
        return pltpu.make_async_copy(
            recent_hbm.at[:, pl.ds(pl.multiple_of(y * 144 + 64, 16), 16), :], mine.at[:, pl.ds(64, 16), :], load_sem.at[12]
        )

    @pl.when(core == 0)
    def _():
        extra().start()

    @pl.when(core == 1)
    def _():
        mine[:, 64:, :] = jnp.zeros((B_DEV, 16, 128), BF)

    barrier = pltpu.get_barrier_semaphore()

    def greet(i, _):
        pl.semaphore_signal(barrier, inc=1, device_id={"branch": lax.rem(me + i, GROUPS)}, device_id_type=MESH)
        return 0

    lax.fori_loop(1, GROUPS, greet, 0)
    for i in range(1, 8):
        pl.semaphore_signal(barrier, inc=1, device_id={"head": lax.rem(head + i, 8)}, device_id_type=MESH)
    for i in range(1, NX):
        for n in range(1, 8):
            pl.semaphore_signal(
                barrier, inc=1,
                device_id={"branch": z * NX + lax.rem(x + i, NX), "head": lax.rem(head + n, 8)},
                device_id_type=MESH,
            )

    loads[0].wait()
    lane = lax.broadcasted_iota(jnp.int32, (1, 128), 1)
    row = jnp.zeros((1, 128), jnp.int32) - 1
    for b in range(0, B_DEV, 2):
        row = jnp.where(lane == b, par[b], row)
    my_par[...] = row
    all_par[me] = row
    pl.semaphore_wait(barrier, GROUPS - 1 + 7 + 21)

    def start_par(i, _):
        d = lax.rem(me + i, GROUPS)
        remote(my_par, all_par.at[me], par_send.at[i], par_recv.at[me], branch=d).start()
        return 0

    lax.fori_loop(1, GROUPS, start_par, 0)

    loads[2].wait()
    loads[3].wait()
    for h in range(HEADS):
        q = dot(qn[:, h * NOPE:(h + 1) * NOPE], ku[h]).astype(BF).astype(F32)
        for j in range(LANES):
            qs[j, pl.ds(h, ROWS, stride=HEADS), :] = q[:, j * 128:(j + 1) * 128]
    loads[4].wait()
    low = lax.broadcasted_iota(jnp.int32, (ROWS, 128), 1) < ROPE
    for h in range(HEADS):
        q = qr[:, (h // 2) * 128:(h // 2 + 1) * 128].astype(F32)
        qs[LANES, pl.ds(h, ROWS, stride=HEADS), :] = jnp.where(low if h % 2 == 0 else ~low, q, 0.0)

    def wait_par(i, _):
        src = lax.rem(me + i, GROUPS)
        remote(my_par, all_par.at[src], par_send.at[i], par_recv.at[src], branch=src).wait()
        return 0

    lax.fori_loop(1, GROUPS, wait_par, 0)
    local = all_par[...] - me * B_DEV
    hit = (local >= 0) & (local < B_DEV)
    pick_v[...] = jnp.broadcast_to(
        jnp.sum(jnp.where(hit, local, 0), axis=2, keepdims=True), (GROUPS, 1, 128)
    )
    pick = pltpu.make_async_copy(pick_v, pick_s, pick_sem)
    pick.start()
    loads[1].wait()

    @pl.when(core == 0)
    def _():
        extra().wait()

    pick.wait()

    def block(n, at, to, size):
        return remote(
            packed.at[n, pl.ds(0, size)], slots.at[at, pl.ds(0, size)], out_send.at[n], out_recv.at[at], branch=to
        )

    for c in range(2):

        @pl.when(core == c)
        def _(c=c):
            def send_block(i, _):
                d = lax.rem(me + i, GROUPS)
                packed[d] = mine[pick_s[d, 0, 0]]
                block(d, me, d, SIZES[c]).start()
                return 0

            lax.fori_loop(1, GROUPS, send_block, 0)

    slots[me] = mine[pick_s[me, 0, 0]]

    for i in range(2 * NX):
        wt[i * PADDED + SLICE:(i + 1) * PADDED, :] = jnp.zeros((PADDED - SLICE, HEADS * VDIM), BF)
    loads[10].wait()
    loads[11].wait()

    def share(m, owner, n, to):
        return remote(columns(owner, n), columns(owner, n), w_send.at[m], w_recv.at[m], branch=z * NX + to)

    for n in range(2):
        share(n, x, n, right).start()
        share(2 + n, x, n, left).start()

    for n in (5, 6, 7, 8):
        loads[n].wait()
    nlt[...] = jnp.zeros_like(nlt)
    nlt[:, :ROWS] = nl[...].astype(F32).T.astype(BF)

    key = lax.broadcasted_iota(jnp.int32, (STEPS * HEADS, 256), 1)
    step = lax.broadcasted_iota(jnp.int32, (STEPS * HEADS, 256), 0) // HEADS

    def query(rows):
        return jnp.concatenate([qs[j, rows, :] for j in range(LANES + 1)], axis=1).astype(BF)

    def scores(rows, keys):
        return dot(query(rows), jnp.concatenate([keys, keys[LAT:]], axis=0))

    def prefix(b, _):
        rows = pl.ds(pl.multiple_of(b * 64, 64), 64)
        keys = jnp.concatenate([pool[table[b]], nlt[...]], axis=1)
        s = scores(rows, keys)
        fresh = key - BLOCK - b * STEPS
        allowed = (key < lens[b]) | ((fresh >= 0) & (fresh <= step))
        s = jnp.where(allowed, s * SCALE, -jnp.inf)
        m = jnp.max(s, axis=1, keepdims=True)
        w = jnp.exp(s - m).astype(BF)
        total[rows, :] = jnp.broadcast_to(jnp.sum(w.astype(F32), axis=1, keepdims=True), (64, 128))
        peak[rows, :] = jnp.broadcast_to(m, (64, 128))
        c = dot_nt(w, keys[:LAT])
        for j in range(LANES):
            ctx[j, rows, :] = c[:, j * 128:(j + 1) * 128]
        return 0

    lax.fori_loop(0, B_DEV // 2, prefix, 0)

    from_down, from_up, from_far = down * 2 + core, up * 2 + core, far * 2 + core
    other = 1 - core

    def piece(h, ch, size, half):
        first, count = (ch * CHUNK, CHUNK) if half is None else (ch * CHUNK + half * (CHUNK // 2), CHUNK // 2)
        return parts.at[h, pl.ds(first, count), pl.ds(0, size)]

    def ring(n, h, ch, size, half, to):
        at = piece(h, ch, size, half)
        return remote(at, at, ring_send.at[ch, n], ring_recv.at[ch, n], head=to * 2 + core)

    def swap(n, h, ch, size, half):
        at = piece(h, ch, size, half)
        return remote(at, at, core_send.at[ch, n], core_recv.at[ch, n], head=y * 2 + other)

    def ring_first(ch, size):
        ring(0, head, ch, size, None, up).start()
        ring(1, head, ch, size, None, down).start()
        swap(0, head, ch, size, None).start()

    def ring_second(ch, size):
        ring(0, from_down, ch, size, None, up).wait()
        ring(2, from_down, ch, size, 0, up).start()
        ring(1, from_up, ch, size, None, down).wait()
        ring(3, from_up, ch, size, 1, down).start()
        swap(1, from_down, ch, size, None).start()
        swap(2, from_up, ch, size, None).start()

    def ring_third(ch, size):
        ring(2, from_far, ch, size, 0, up).wait()
        swap(3, from_far, ch, size, 0).start()
        ring(3, from_far, ch, size, 1, down).wait()
        swap(4, from_far, ch, size, 1).start()

    def ring_end(ch, size, other_size):
        for n, h, half in ((0, head, None), (1, from_down, None), (2, from_up, None), (3, from_far, 0), (4, from_far, 1)):
            swap(n, h, ch, size, half).wait_send()
            swap(n, h + other - core, ch, other_size, half).wait_recv()

    for c in range(2):

        @pl.when(core == c)
        def _(c=c):
            def wait_block(i, _):
                src = lax.rem(me + i, GROUPS)
                block(src, src, src, SIZES[c]).wait()
                return 0

            lax.fori_loop(1, GROUPS, wait_block, 0)
            for ch in range(2):
                for p in range(ch * CHUNK, (ch + 1) * CHUNK):
                    parts[head, p] = slots[par[2 * p] // B_DEV]
                ring_first(ch, SIZES[c])

    lax.fori_loop(B_DEV // 2, B_DEV, prefix, 0)

    for c in range(2):

        @pl.when(core == c)
        def _(c=c):
            ring_second(0, SIZES[c])
            ring_second(1, SIZES[c])
            ring_third(0, SIZES[c])
            ring_third(1, SIZES[c])

    share(0, left, 0, right).wait()
    share(4, left, 0, right).start()
    share(3, right, 1, left).wait()
    share(5, right, 1, left).start()
    share(1, left, 1, right).wait()
    share(2, right, 0, left).wait()

    def arrive(ch):
        for c in range(2):

            @pl.when(core == c)
            def _(c=c):
                ring_end(ch, SIZES[c], SIZES[1 - c])

        def gather(p, _):
            for yy in range(NY):
                fork[p, yy * 144:yy * 144 + 80] = parts[2 * yy, p]
                fork[p, yy * 144 + 80:yy * 144 + 144] = parts[2 * yy + 1, p, :64]
            return 0

        lax.fori_loop(ch * CHUNK, (ch + 1) * CHUNK, gather, 0)

    def forked(n, _):
        several = range(TOGETHER)
        rows = [pl.ds(pl.multiple_of((n * TOGETHER + i) * 128, 128), 128) for i in several]
        keys = [fork[n * TOGETHER + i] for i in several]
        s = [scores(rows[i], keys[i]) * SCALE for i in several]
        old = [peak[rows[i], :][:, :1] for i in several]
        m = [jnp.maximum(jnp.max(s[i], axis=1, keepdims=True), old[i]) for i in several]
        w = [jnp.exp(s[i] - m[i]).astype(BF) for i in several]
        back = [jnp.exp(old[i] - m[i]) for i in several]
        norm = [
            total[rows[i], :][:, :1] * back[i] + jnp.sum(w[i].astype(F32), axis=1, keepdims=True) for i in several
        ]
        c = [dot_nt(w[i], keys[i][:LAT]) for i in several]
        scale = [1.0 / norm[i] for i in several]
        both = [
            [(ctx[j, rows[i], :] * back[i] + c[i][:, j * 128:(j + 1) * 128]) * scale[i] for j in range(LANES)]
            for i in several
        ]
        for i in several:
            for j in range(LANES):
                ctx[j, rows[i], :] = both[i][j].astype(BF).astype(F32)
        return 0

    def half_of(slot, s):
        return held.at[slot, pl.ds(s * HALF, HALF)]

    def hop(way, k, s):
        came, goes = (k - 1, k) if way == 0 else ((9 - k) % 8, 8 - k)
        return remote(
            half_of(came, s), half_of(goes, s), z_send.at[way, k - 1, s], z_recv.at[way, k - 1, s],
            branch=nxt if way == 0 else prv,
        )

    hops = []

    def go(way, k, s):
        c = hop(way, k, s)
        c.start()
        hops.append(c)

    loads[9].wait()
    for s in (0, 1):
        arrive(s)
        lax.fori_loop(s * (PAIRS // 2) // TOGETHER, (s + 1) * (PAIRS // 2) // TOGETHER, forked, 0)
        for h in range(HEADS):
            c = [ctx[j, pl.ds(s * HALF * HEADS + h, HALF, stride=HEADS), :] for j in range(LANES)]
            c = jnp.concatenate(c, axis=1).astype(BF)
            held[0, s * HALF:(s + 1) * HALF, h * VDIM:(h + 1) * VDIM] = dot(c, vu[h]).astype(BF)
        go(0, 1, s)
        go(1, 1, s)

    share(4, lax.rem(x + 2, NX), 0, right).wait()
    share(5, lax.rem(x + 2, NX), 1, left).wait()

    def swap_sums(slot):
        return remote(made.at[slot, other], met.at[slot], r_send.at[slot], r_recv.at[slot], head=y * 2 + other)

    def multiply(slot):
        for i in range(NX):
            r = dot_nt(held[slot], wt[i * 2 * PADDED:(i + 1) * 2 * PADDED]).astype(BF)
            for n in range(2):
                made[slot, n, i] = r[:, n * PADDED:(n + 1) * PADDED]
        swap_sums(slot).start()

    def deliver(slot, i):
        return remote(
            summed.at[slot, i], landed.at[x, head], f_send.at[slot, i], f_recv.at[x, head],
            branch=z * NX + i, head=lax.rem(z + 8 - slot, 8),
        )

    def stays(slot, i):
        return (i == x) & (lax.rem(z + 8 - slot, 8) == head)

    def fold(slot):
        swap_sums(slot).wait_recv()
        for i in range(NX):
            both = (made[slot, core, i].astype(F32) + met[slot, i].astype(F32)).astype(BF)
            summed[slot, i] = both
            here = stays(slot, i)

            @pl.when(here)
            def _(both=both):
                landed[x, head] = both

            @pl.when(~here)
            def _(i=i):
                deliver(slot, i).start()

    order = (0, 1, 7, 2, 6, 3, 5, 4)

    def turn(slot):
        n = order.index(slot)
        multiply(slot)
        if n >= 1:
            fold(order[n - 1])

    turn(0)
    for k in (1, 2, 3):
        for s in (0, 1):
            for way in (0, 1):
                t = s if way == 0 else 1 - s
                hop(way, k, t).wait_recv()
                if k < 3 or t == way:
                    go(way, k + 1, t)
            if s == 0 and k > 1:
                turn(9 - k)
        turn(k)
    turn(5)
    hop(0, 4, 0).wait_recv()
    hop(1, 4, 1).wait_recv()
    turn(4)
    fold(4)

    for i in range(NX):
        sides = []
        for n in range(2):
            acc = jnp.zeros((ROWS, PADDED), F32)
            for yy in range(NY):
                src = 2 * yy + n

                @pl.when((i != x) | (src != head))
                def _(i=i, src=src):
                    remote(
                        summed.at[0, 0], landed.at[i, src], f_send.at[0, 0], f_recv.at[i, src],
                        branch=z * NX + i, head=src,
                    ).wait_recv()

                acc = acc + landed[i, src].astype(F32)
            sides.append(acc.astype(BF)[:, :SLICE])
        out[i * ROWS:(i + 1) * ROWS, :] = jnp.concatenate(sides, axis=1)

    for c in hops:
        c.wait_send()
    for slot in range(8):
        swap_sums(slot).wait_send()
        for i in range(NX):

            @pl.when(~stays(slot, i))
            def _(slot=slot, i=i):
                deliver(slot, i).wait_send()


def layer(*operands):
    vmem, dma = pltpu.VMEM, pltpu.SemaphoreType.DMA
    smem = pltpu.SMEM
    return pl.pallas_call(
        layer_kernel,
        out_shape=jax.ShapeDtypeStruct((NX * ROWS, COLS), BF),
        in_specs=[pl.BlockSpec(memory_space=pl.ANY)] * 11,
        out_specs=pl.BlockSpec(memory_space=pltpu.VMEM),
        scratch_shapes=[
            smem((B_DEV,), jnp.int32), smem((B_DEV,), jnp.int32), smem((B_DEV,), jnp.int32),
            vmem((ROWS, HEADS * NOPE), BF),
            vmem((ROWS, HEADS * ROPE), BF),
            vmem((HEADS, NOPE, LAT), BF),
            vmem((HEADS, LAT, VDIM), BF),
            vmem((B_DEV, WIDTH, BLOCK), BF),
            vmem((ROWS, WIDTH), BF),
            vmem((WIDTH, 128), BF),
            vmem((2 * NX * PADDED, HEADS * VDIM), BF),
            vmem((LANES + 1, QROWS, 128), F32),
            vmem((LANES, QROWS, 128), F32),
            vmem((QROWS, 128), F32),
            vmem((QROWS, 128), F32),
            vmem((B_DEV, PART, 128), BF),
            vmem((GROUPS, PART, 128), BF),
            vmem((GROUPS, PART, 128), BF),
            vmem((1, 128), jnp.int32),
            vmem((GROUPS, 1, 128), jnp.int32),
            vmem((GROUPS, 1, 128), jnp.int32),
            smem((GROUPS, 1, 128), jnp.int32),
            vmem((8, PAIRS, PART, 128), BF),
            vmem((PAIRS, WIDTH, BLOCK), BF),
            vmem((8, ROWS, HEADS * VDIM), BF),
            vmem((8, 2, NY, ROWS, PADDED), BF),
            vmem((8, NX, ROWS, PADDED), BF),
            vmem((8, NX, ROWS, PADDED), BF),
            vmem((NX, 8, ROWS, PADDED), BF),
            dma((13,)), dma,
            dma((GROUPS,)), dma((GROUPS,)), dma((GROUPS,)), dma((GROUPS,)),
            dma((2, 4)), dma((2, 4)), dma((2, 5)), dma((2, 5)),
            dma((6,)), dma((6,)), dma((2, 4, 2)), dma((2, 4, 2)), dma((8,)), dma((8,)), dma((8, NX)), dma((NX, 8)),
        ],
        compiler_params=pltpu.CompilerParams(
            collective_id=0, has_side_effects=True, vmem_limit_bytes=VMEM_BYTES
        ),
        cost_estimate=pl.CostEstimate(flops=4_200_000_000, bytes_accessed=16_000_000, transcendentals=400_000),
    )(*operands)


def local(
    query_nope, query_rope, key_up, value_up, out_weight, block_pool, recent_blocks, new_latent,
    parent, lengths, block_table,
):
    return layer(
        parent, lengths, block_table.reshape(B_DEV), query_nope, query_rope, key_up, value_up,
        jnp.swapaxes(block_pool, 1, 2), jnp.swapaxes(recent_blocks, 1, 2), new_latent, out_weight.T,
    )


def solution(mesh):
    return jax.shard_map(
        local,
        mesh=mesh,
        in_specs=(
            P("branch", "head"),
            P("branch", "head"),
            P("head", None, None),
            P("head", None, None),
            P("head", "branch"),
            P("branch", None, None),
            P("branch", None, None),
            P("branch", None),
            P("branch"),
            P("branch"),
            P("branch", None),
        ),
        out_specs=P("head", "branch"),
        check_vma=False,
    )
```

```python
import functools

import jax
import jax.numpy as jnp
from jax import lax
from jax.experimental import pallas as pl
from jax.experimental.pallas import tpu as pltpu
from jax.sharding import PartitionSpec as P

NOPE = 128
ROPE = 64
LAT = 512
VDIM = 128
BLOCK = 128
STEPS = 4
B_DEV = 24
PAIRS = B_DEV // 2
WIDTH = LAT + ROPE
HEADS = 16
ROWS = B_DEV * STEPS
HALF = ROWS // 2
QROWS = ROWS * HEADS
COLS = 224
NZ, NX, NY = 8, 4, 4
GROUPS = NZ * NX
PART = 80
CHUNK = PAIRS // 2
SLICE = COLS // 2
PADDED = 128
VMEM_BYTES = 60 * 2**20
LANES = LAT // 128
TOGETHER = 3
EARLY = 20
SCALE = (NOPE + ROPE) ** -0.5
BF = jnp.bfloat16
F32 = jnp.float32
MESH = pl.DeviceIdType.MESH
NT = (((1,), (1,)), ((), ()))


SIZES = (80, 64)


def dot(a, b):
    return jnp.dot(a, b, preferred_element_type=F32)


def dot_nt(a, b):
    return lax.dot_general(a, b, NT, preferred_element_type=F32)


def remote(src, dst, send, recv, **where):
    return pltpu.make_async_remote_copy(
        src_ref=src, dst_ref=dst, send_sem=send, recv_sem=recv,
        device_id=where, device_id_type=MESH,
    )


def layer_kernel(
    par_hbm, lens_hbm, table_hbm,
    qn_hbm, qr_hbm, ku_hbm, vu_hbm, pool_hbm, recent_hbm, nl_hbm, w_hbm,
    out,
    par, lens, table,
    qn, qr, ku, vu, pool, nl, nlt, wt,
    qs, ctx, peak, total,
    mine, packed, slots, my_par, all_par, pick_v, pick_s, parts, fork,
    held, made, met, summed, landed,
    load_sem, pick_sem, par_send, par_recv, out_send, out_recv, ring_send, ring_recv, core_send, core_recv,
    w_send, w_recv, z_send, z_recv, r_send, r_recv, f_send, f_recv,
):
    me = lax.axis_index("branch")
    head = lax.axis_index("head")
    z, x = me // NX, lax.rem(me, NX)
    y, core = head // 2, lax.rem(head, 2)
    up, down = lax.rem(y + 1, NY), lax.rem(y + 3, NY)
    far = lax.rem(y + 2, NY)
    left, right = lax.rem(x + 3, NX), lax.rem(x + 1, NX)
    nxt = lax.rem(z + 1, NZ) * NX + x
    prv = lax.rem(z + NZ - 1, NZ) * NX + x
    row0 = pl.multiple_of(y * 144 + core * PART, 16)

    def columns(i, n):
        return wt.at[pl.ds(pl.multiple_of((2 * i + n) * PADDED, PADDED), SLICE)]

    pairs = (
        (par_hbm, par), (recent_hbm.at[:, pl.ds(row0, 64), :], mine.at[:, pl.ds(0, 64), :]), (ku_hbm, ku), (qn_hbm, qn), (qr_hbm, qr),
        (lens_hbm, lens), (table_hbm, table), (pool_hbm, pool), (nl_hbm, nl), (vu_hbm, vu), (w_hbm.at[pl.ds(0, SLICE)], columns(x, 0)),
        (w_hbm.at[pl.ds(SLICE, SLICE)], columns(x, 1)),
    )
    loads = [pltpu.make_async_copy(src, dst, load_sem.at[i]) for i, (src, dst) in enumerate(pairs)]
    for load in loads:
        load.start()

    def extra():
        return pltpu.make_async_copy(
            recent_hbm.at[:, pl.ds(pl.multiple_of(y * 144 + 64, 16), 16), :], mine.at[:, pl.ds(64, 16), :], load_sem.at[12]
        )

    @pl.when(core == 0)
    def _():
        extra().start()

    @pl.when(core == 1)
    def _():
        mine[:, 64:, :] = jnp.zeros((B_DEV, 16, 128), BF)

    barrier = pltpu.get_barrier_semaphore()

    def greet(i, _):
        pl.semaphore_signal(barrier, inc=1, device_id={"branch": lax.rem(me + i, GROUPS)}, device_id_type=MESH)
        return 0

    lax.fori_loop(1, GROUPS, greet, 0)
    for i in range(1, 8):
        pl.semaphore_signal(barrier, inc=1, device_id={"head": lax.rem(head + i, 8)}, device_id_type=MESH)
    for i in range(1, NX):
        for n in range(1, 8):
            pl.semaphore_signal(
                barrier, inc=1,
                device_id={"branch": z * NX + lax.rem(x + i, NX), "head": lax.rem(head + n, 8)},
                device_id_type=MESH,
            )

    loads[0].wait()
    lane = lax.broadcasted_iota(jnp.int32, (1, 128), 1)
    row = jnp.zeros((1, 128), jnp.int32) - 1
    for b in range(0, B_DEV, 2):
        row = jnp.where(lane == b, par[b], row)
    my_par[...] = row
    all_par[me] = row
    pl.semaphore_wait(barrier, GROUPS - 1 + 7 + 21)

    def start_par(i, _):
        d = lax.rem(me + i, GROUPS)
        remote(my_par, all_par.at[me], par_send.at[i], par_recv.at[me], branch=d).start()
        return 0

    lax.fori_loop(1, GROUPS, start_par, 0)

    loads[2].wait()
    loads[3].wait()
    for h in range(HEADS):
        q = dot(qn[:, h * NOPE:(h + 1) * NOPE], ku[h]).astype(BF).astype(F32)
        for j in range(LANES):
            qs[j, pl.ds(h, ROWS, stride=HEADS), :] = q[:, j * 128:(j + 1) * 128]
    loads[4].wait()
    low = lax.broadcasted_iota(jnp.int32, (ROWS, 128), 1) < ROPE
    for h in range(HEADS):
        q = qr[:, (h // 2) * 128:(h // 2 + 1) * 128].astype(F32)
        qs[LANES, pl.ds(h, ROWS, stride=HEADS), :] = jnp.where(low if h % 2 == 0 else ~low, q, 0.0)

    def wait_par(i, _):
        src = lax.rem(me + i, GROUPS)
        remote(my_par, all_par.at[src], par_send.at[i], par_recv.at[src], branch=src).wait()
        return 0

    lax.fori_loop(1, GROUPS, wait_par, 0)
    local = all_par[...] - me * B_DEV
    hit = (local >= 0) & (local < B_DEV)
    pick_v[...] = jnp.broadcast_to(
        jnp.sum(jnp.where(hit, local, 0), axis=2, keepdims=True), (GROUPS, 1, 128)
    )
    pick = pltpu.make_async_copy(pick_v, pick_s, pick_sem)
    pick.start()
    loads[1].wait()

    @pl.when(core == 0)
    def _():
        extra().wait()

    pick.wait()

    def block(n, at, to, size):
        return remote(
            packed.at[n, pl.ds(0, size)], slots.at[at, pl.ds(0, size)], out_send.at[n], out_recv.at[at], branch=to
        )

    for c in range(2):

        @pl.when(core == c)
        def _(c=c):
            def send_block(i, _):
                d = lax.rem(me + i, GROUPS)
                packed[d] = mine[pick_s[d, 0, 0]]
                block(d, me, d, SIZES[c]).start()
                return 0

            lax.fori_loop(1, GROUPS, send_block, 0)

    slots[me] = mine[pick_s[me, 0, 0]]

    for i in range(2 * NX):
        wt[i * PADDED + SLICE:(i + 1) * PADDED, :] = jnp.zeros((PADDED - SLICE, HEADS * VDIM), BF)
    loads[10].wait()
    loads[11].wait()

    def share(m, owner, n, to):
        return remote(columns(owner, n), columns(owner, n), w_send.at[m], w_recv.at[m], branch=z * NX + to)

    for n in range(2):
        share(n, x, n, right).start()
        share(2 + n, x, n, left).start()

    for n in (5, 6, 7, 8):
        loads[n].wait()
    nlt[...] = jnp.zeros_like(nlt)
    nlt[:, :ROWS] = nl[...].astype(F32).T.astype(BF)

    key = lax.broadcasted_iota(jnp.int32, (STEPS * HEADS, 256), 1)
    step = lax.broadcasted_iota(jnp.int32, (STEPS * HEADS, 256), 0) // HEADS

    def query(rows):
        return jnp.concatenate([qs[j, rows, :] for j in range(LANES + 1)], axis=1).astype(BF)

    def scores(rows, keys):
        return dot(query(rows), jnp.concatenate([keys, keys[LAT:]], axis=0))

    def prefix(b, _):
        rows = pl.ds(pl.multiple_of(b * 64, 64), 64)
        keys = jnp.concatenate([pool[table[b]], nlt[...]], axis=1)
        s = scores(rows, keys)
        fresh = key - BLOCK - b * STEPS
        allowed = (key < lens[b]) | ((fresh >= 0) & (fresh <= step))
        s = jnp.where(allowed, s * SCALE, -jnp.inf)
        m = jnp.max(s, axis=1, keepdims=True)
        w = jnp.exp(s - m).astype(BF)
        total[rows, :] = jnp.broadcast_to(jnp.sum(w.astype(F32), axis=1, keepdims=True), (64, 128))
        peak[rows, :] = jnp.broadcast_to(m, (64, 128))
        c = dot_nt(w, keys[:LAT])
        for j in range(LANES):
            ctx[j, rows, :] = c[:, j * 128:(j + 1) * 128]
        return 0

    lax.fori_loop(0, EARLY, prefix, 0)

    from_down, from_up, from_far = down * 2 + core, up * 2 + core, far * 2 + core
    other = 1 - core

    def piece(h, ch, size, half):
        first, count = (ch * CHUNK, CHUNK) if half is None else (ch * CHUNK + half * (CHUNK // 2), CHUNK // 2)
        return parts.at[h, pl.ds(first, count), pl.ds(0, size)]

    def ring(n, h, ch, size, half, to):
        at = piece(h, ch, size, half)
        return remote(at, at, ring_send.at[ch, n], ring_recv.at[ch, n], head=to * 2 + core)

    def swap(n, h, ch, size, half):
        at = piece(h, ch, size, half)
        return remote(at, at, core_send.at[ch, n], core_recv.at[ch, n], head=y * 2 + other)

    def ring_first(ch, size):
        ring(0, head, ch, size, None, up).start()
        ring(1, head, ch, size, None, down).start()
        swap(0, head, ch, size, None).start()

    def ring_second(ch, size):
        ring(0, from_down, ch, size, None, up).wait()
        ring(2, from_down, ch, size, 0, up).start()
        ring(1, from_up, ch, size, None, down).wait()
        ring(3, from_up, ch, size, 1, down).start()
        swap(1, from_down, ch, size, None).start()
        swap(2, from_up, ch, size, None).start()

    def ring_third(ch, size):
        ring(2, from_far, ch, size, 0, up).wait()
        swap(3, from_far, ch, size, 0).start()
        ring(3, from_far, ch, size, 1, down).wait()
        swap(4, from_far, ch, size, 1).start()

    def ring_end(ch, size, other_size):
        for n, h, half in ((0, head, None), (1, from_down, None), (2, from_up, None), (3, from_far, 0), (4, from_far, 1)):
            swap(n, h, ch, size, half).wait_send()
            swap(n, h + other - core, ch, other_size, half).wait_recv()

    for c in range(2):

        @pl.when(core == c)
        def _(c=c):
            def wait_block(i, _):
                src = lax.rem(me + i, GROUPS)
                block(src, src, src, SIZES[c]).wait()
                return 0

            lax.fori_loop(1, GROUPS, wait_block, 0)
            for ch in range(2):
                for p in range(ch * CHUNK, (ch + 1) * CHUNK):
                    parts[head, p] = slots[par[2 * p] // B_DEV]
                ring_first(ch, SIZES[c])

    lax.fori_loop(EARLY, B_DEV, prefix, 0)

    for c in range(2):

        @pl.when(core == c)
        def _(c=c):
            ring_second(0, SIZES[c])
            ring_second(1, SIZES[c])
            ring_third(0, SIZES[c])
            ring_third(1, SIZES[c])

    share(0, left, 0, right).wait()
    share(4, left, 0, right).start()
    share(3, right, 1, left).wait()
    share(5, right, 1, left).start()
    share(1, left, 1, right).wait()
    share(2, right, 0, left).wait()

    def arrive(ch):
        for c in range(2):

            @pl.when(core == c)
            def _(c=c):
                ring_end(ch, SIZES[c], SIZES[1 - c])

        def gather(p, _):
            for yy in range(NY):
                fork[p, yy * 144:yy * 144 + 80] = parts[2 * yy, p]
                fork[p, yy * 144 + 80:yy * 144 + 144] = parts[2 * yy + 1, p, :64]
            return 0

        lax.fori_loop(ch * CHUNK, (ch + 1) * CHUNK, gather, 0)

    def forked(n, _):
        several = range(TOGETHER)
        rows = [pl.ds(pl.multiple_of((n * TOGETHER + i) * 128, 128), 128) for i in several]
        keys = [fork[n * TOGETHER + i] for i in several]
        s = [scores(rows[i], keys[i]) * SCALE for i in several]
        old = [peak[rows[i], :][:, :1] for i in several]
        m = [jnp.maximum(jnp.max(s[i], axis=1, keepdims=True), old[i]) for i in several]
        w = [jnp.exp(s[i] - m[i]).astype(BF) for i in several]
        back = [jnp.exp(old[i] - m[i]) for i in several]
        norm = [
            total[rows[i], :][:, :1] * back[i] + jnp.sum(w[i].astype(F32), axis=1, keepdims=True) for i in several
        ]
        c = [dot_nt(w[i], keys[i][:LAT]) for i in several]
        scale = [1.0 / norm[i] for i in several]
        both = [
            [(ctx[j, rows[i], :] * back[i] + c[i][:, j * 128:(j + 1) * 128]) * scale[i] for j in range(LANES)]
            for i in several
        ]
        for i in several:
            for j in range(LANES):
                ctx[j, rows[i], :] = both[i][j].astype(BF).astype(F32)
        return 0

    def half_of(slot, s):
        return held.at[slot, pl.ds(s * HALF, HALF)]

    def hop(way, k, s):
        came, goes = (k - 1, k) if way == 0 else ((9 - k) % 8, 8 - k)
        return remote(
            half_of(came, s), half_of(goes, s), z_send.at[way, k - 1, s], z_recv.at[way, k - 1, s],
            branch=nxt if way == 0 else prv,
        )

    hops = []

    def go(way, k, s):
        c = hop(way, k, s)
        c.start()
        hops.append(c)

    loads[9].wait()
    for s in (0, 1):
        arrive(s)
        lax.fori_loop(s * (PAIRS // 2) // TOGETHER, (s + 1) * (PAIRS // 2) // TOGETHER, forked, 0)
        for h in range(HEADS):
            c = [ctx[j, pl.ds(s * HALF * HEADS + h, HALF, stride=HEADS), :] for j in range(LANES)]
            c = jnp.concatenate(c, axis=1).astype(BF)
            held[0, s * HALF:(s + 1) * HALF, h * VDIM:(h + 1) * VDIM] = dot(c, vu[h]).astype(BF)
        go(0, 1, s)
        go(1, 1, s)

    share(4, lax.rem(x + 2, NX), 0, right).wait()
    share(5, lax.rem(x + 2, NX), 1, left).wait()

    def swap_sums(slot, i):
        return remote(
            made.at[slot, other, i], met.at[slot, i], r_send.at[slot, i], r_recv.at[slot, i], head=y * 2 + other
        )

    def multiply(slot):
        for i in range(NX):
            r = dot_nt(held[slot], wt[i * 2 * PADDED:(i + 1) * 2 * PADDED]).astype(BF)
            for n in range(2):
                made[slot, n, i] = r[:, n * PADDED:(n + 1) * PADDED]
            swap_sums(slot, i).start()

    def deliver(slot, i):
        return remote(
            summed.at[slot, i], landed.at[x, head], f_send.at[slot, i], f_recv.at[x, head],
            branch=z * NX + i, head=lax.rem(z + 8 - slot, 8),
        )

    def stays(slot, i):
        return (i == x) & (lax.rem(z + 8 - slot, 8) == head)

    def fold(slot):
        for i in range(NX):
            swap_sums(slot, i).wait_recv()
            both = (made[slot, core, i].astype(F32) + met[slot, i].astype(F32)).astype(BF)
            summed[slot, i] = both
            here = stays(slot, i)

            @pl.when(here)
            def _(both=both):
                landed[x, head] = both

            @pl.when(~here)
            def _(i=i):
                deliver(slot, i).start()

    order = (0, 1, 7, 2, 6, 3, 5, 4)

    def turn(slot):
        n = order.index(slot)
        multiply(slot)
        if 1 <= n < 7:
            fold(order[n - 1])

    turn(0)
    for k in (1, 2, 3):
        for s in (0, 1):
            for way in (0, 1):
                t = s if way == 0 else 1 - s
                hop(way, k, t).wait_recv()
                if k < 3 or t == way:
                    go(way, k + 1, t)
            if s == 0 and k > 1:
                turn(9 - k)
        turn(k)
    turn(5)
    fold(5)
    hop(0, 4, 0).wait_recv()
    hop(1, 4, 1).wait_recv()
    turn(4)
    fold(4)

    for i in range(NX):
        sides = []
        for n in range(2):
            acc = jnp.zeros((ROWS, PADDED), F32)
            for yy in range(NY):
                src = 2 * yy + n

                @pl.when((i != x) | (src != head))
                def _(i=i, src=src):
                    remote(
                        summed.at[0, 0], landed.at[i, src], f_send.at[0, 0], f_recv.at[i, src],
                        branch=z * NX + i, head=src,
                    ).wait_recv()

                acc = acc + landed[i, src].astype(F32)
            sides.append(acc.astype(BF)[:, :SLICE])
        out[i * ROWS:(i + 1) * ROWS, :] = jnp.concatenate(sides, axis=1)

    for c in hops:
        c.wait_send()
    for slot in range(8):
        for i in range(NX):
            swap_sums(slot, i).wait_send()

            @pl.when(~stays(slot, i))
            def _(slot=slot, i=i):
                deliver(slot, i).wait_send()


def layer(*operands):
    vmem, dma = pltpu.VMEM, pltpu.SemaphoreType.DMA
    smem = pltpu.SMEM
    return pl.pallas_call(
        layer_kernel,
        out_shape=jax.ShapeDtypeStruct((NX * ROWS, COLS), BF),
        in_specs=[pl.BlockSpec(memory_space=pl.ANY)] * 11,
        out_specs=pl.BlockSpec(memory_space=pltpu.VMEM),
        scratch_shapes=[
            smem((B_DEV,), jnp.int32), smem((B_DEV,), jnp.int32), smem((B_DEV,), jnp.int32),
            vmem((ROWS, HEADS * NOPE), BF),
            vmem((ROWS, HEADS * ROPE), BF),
            vmem((HEADS, NOPE, LAT), BF),
            vmem((HEADS, LAT, VDIM), BF),
            vmem((B_DEV, WIDTH, BLOCK), BF),
            vmem((ROWS, WIDTH), BF),
            vmem((WIDTH, 128), BF),
            vmem((2 * NX * PADDED, HEADS * VDIM), BF),
            vmem((LANES + 1, QROWS, 128), F32),
            vmem((LANES, QROWS, 128), F32),
            vmem((QROWS, 128), F32),
            vmem((QROWS, 128), F32),
            vmem((B_DEV, PART, 128), BF),
            vmem((GROUPS, PART, 128), BF),
            vmem((GROUPS, PART, 128), BF),
            vmem((1, 128), jnp.int32),
            vmem((GROUPS, 1, 128), jnp.int32),
            vmem((GROUPS, 1, 128), jnp.int32),
            smem((GROUPS, 1, 128), jnp.int32),
            vmem((8, PAIRS, PART, 128), BF),
            vmem((PAIRS, WIDTH, BLOCK), BF),
            vmem((8, ROWS, HEADS * VDIM), BF),
            vmem((8, 2, NY, ROWS, PADDED), BF),
            vmem((8, NX, ROWS, PADDED), BF),
            vmem((8, NX, ROWS, PADDED), BF),
            vmem((NX, 8, ROWS, PADDED), BF),
            dma((13,)), dma,
            dma((GROUPS,)), dma((GROUPS,)), dma((GROUPS,)), dma((GROUPS,)),
            dma((2, 4)), dma((2, 4)), dma((2, 5)), dma((2, 5)),
            dma((6,)), dma((6,)), dma((2, 4, 2)), dma((2, 4, 2)), dma((8, NX)), dma((8, NX)), dma((8, NX)), dma((NX, 8)),
        ],
        compiler_params=pltpu.CompilerParams(
            collective_id=0, has_side_effects=True, vmem_limit_bytes=VMEM_BYTES
        ),
        cost_estimate=pl.CostEstimate(flops=4_200_000_000, bytes_accessed=16_000_000, transcendentals=400_000),
    )(*operands)


def local(
    query_nope, query_rope, key_up, value_up, out_weight, block_pool, recent_blocks, new_latent,
    parent, lengths, block_table,
):
    return layer(
        parent, lengths, block_table.reshape(B_DEV), query_nope, query_rope, key_up, value_up,
        jnp.swapaxes(block_pool, 1, 2), jnp.swapaxes(recent_blocks, 1, 2), new_latent, out_weight.T,
    )


def solution(mesh):
    return jax.shard_map(
        local,
        mesh=mesh,
        in_specs=(
            P("branch", "head"),
            P("branch", "head"),
            P("head", None, None),
            P("head", None, None),
            P("head", "branch"),
            P("branch", None, None),
            P("branch", None, None),
            P("branch", None),
            P("branch"),
            P("branch"),
            P("branch", None),
        ),
        out_specs=P("head", "branch"),
        check_vma=False,
    )
```

```python
import functools

import jax
import jax.numpy as jnp
from jax import lax
from jax.experimental import pallas as pl
from jax.experimental.pallas import tpu as pltpu
from jax.sharding import PartitionSpec as P

NOPE = 128
ROPE = 64
LAT = 512
VDIM = 128
BLOCK = 128
STEPS = 4
B_DEV = 24
PAIRS = B_DEV // 2
WIDTH = LAT + ROPE
HEADS = 16
ROWS = B_DEV * STEPS
HALF = ROWS // 2
QROWS = ROWS * HEADS
COLS = 224
NZ, NX, NY = 8, 4, 4
GROUPS = NZ * NX
PART = 80
CHUNK = PAIRS // 2
SLICE = COLS // 2
PADDED = 128
VMEM_BYTES = 60 * 2**20
LANES = LAT // 128
TOGETHER = 3
EARLY = 20
SCALE = (NOPE + ROPE) ** -0.5
BF = jnp.bfloat16
F32 = jnp.float32
MESH = pl.DeviceIdType.MESH
NT = (((1,), (1,)), ((), ()))


SIZES = (80, 64)


def dot(a, b):
    return jnp.dot(a, b, preferred_element_type=F32)


def dot_nt(a, b):
    return lax.dot_general(a, b, NT, preferred_element_type=F32)


def remote(src, dst, send, recv, **where):
    return pltpu.make_async_remote_copy(
        src_ref=src, dst_ref=dst, send_sem=send, recv_sem=recv,
        device_id=where, device_id_type=MESH,
    )


def layer_kernel(
    par_hbm, lens_hbm, table_hbm,
    qn_hbm, qr_hbm, ku_hbm, vu_hbm, pool_hbm, recent_hbm, nl_hbm, w_hbm,
    out,
    par, lens, table,
    qn, qr, ku, vu, pool, nl, nlt, wt,
    qs, ctx, peak, total,
    mine, packed, slots, my_par, all_par, pick_v, pick_s, parts, fork,
    held, made, met, summed, landed,
    load_sem, pick_sem, par_send, par_recv, out_send, out_recv, ring_send, ring_recv, core_send, core_recv,
    w_send, w_recv, z_send, z_recv, r_send, r_recv, f_send, f_recv,
):
    me = lax.axis_index("branch")
    head = lax.axis_index("head")
    z, x = me // NX, lax.rem(me, NX)
    y, core = head // 2, lax.rem(head, 2)
    up, down = lax.rem(y + 1, NY), lax.rem(y + 3, NY)
    far = lax.rem(y + 2, NY)
    left, right = lax.rem(x + 3, NX), lax.rem(x + 1, NX)
    nxt = lax.rem(z + 1, NZ) * NX + x
    prv = lax.rem(z + NZ - 1, NZ) * NX + x
    row0 = pl.multiple_of(y * 144 + core * PART, 16)

    def columns(i, n):
        return wt.at[pl.ds(pl.multiple_of((2 * i + n) * PADDED, PADDED), SLICE)]

    pairs = (
        (par_hbm, par), (recent_hbm.at[:, pl.ds(row0, 64), :], mine.at[:, pl.ds(0, 64), :]), (ku_hbm, ku), (qn_hbm, qn), (qr_hbm, qr),
        (lens_hbm, lens), (table_hbm, table), (pool_hbm, pool), (nl_hbm, nl), (vu_hbm, vu), (w_hbm.at[pl.ds(0, SLICE)], columns(x, 0)),
        (w_hbm.at[pl.ds(SLICE, SLICE)], columns(x, 1)),
    )
    loads = [pltpu.make_async_copy(src, dst, load_sem.at[i]) for i, (src, dst) in enumerate(pairs)]
    for load in loads:
        load.start()

    def extra():
        return pltpu.make_async_copy(
            recent_hbm.at[:, pl.ds(pl.multiple_of(y * 144 + 64, 16), 16), :], mine.at[:, pl.ds(64, 16), :], load_sem.at[12]
        )

    @pl.when(core == 0)
    def _():
        extra().start()

    @pl.when(core == 1)
    def _():
        mine[:, 64:, :] = jnp.zeros((B_DEV, 16, 128), BF)

    barrier = pltpu.get_barrier_semaphore()

    def greet(i, _):
        pl.semaphore_signal(barrier, inc=1, device_id={"branch": lax.rem(me + i, GROUPS)}, device_id_type=MESH)
        return 0

    lax.fori_loop(1, GROUPS, greet, 0)
    for i in range(1, 8):
        pl.semaphore_signal(barrier, inc=1, device_id={"head": lax.rem(head + i, 8)}, device_id_type=MESH)
    for i in range(1, NX):
        for n in range(1, 8):
            pl.semaphore_signal(
                barrier, inc=1,
                device_id={"branch": z * NX + lax.rem(x + i, NX), "head": lax.rem(head + n, 8)},
                device_id_type=MESH,
            )

    loads[0].wait()
    lane = lax.broadcasted_iota(jnp.int32, (1, 128), 1)
    row = jnp.zeros((1, 128), jnp.int32) - 1
    for b in range(0, B_DEV, 2):
        row = jnp.where(lane == b, par[b], row)
    my_par[...] = row
    all_par[me] = row
    pl.semaphore_wait(barrier, GROUPS - 1 + 7 + 21)

    def start_par(i, _):
        d = lax.rem(me + i, GROUPS)
        remote(my_par, all_par.at[me], par_send.at[i], par_recv.at[me], branch=d).start()
        return 0

    lax.fori_loop(1, GROUPS, start_par, 0)

    loads[2].wait()
    loads[3].wait()
    for h in range(HEADS):
        q = dot(qn[:, h * NOPE:(h + 1) * NOPE], ku[h]).astype(BF).astype(F32)
        for j in range(LANES):
            qs[j, pl.ds(h, ROWS, stride=HEADS), :] = q[:, j * 128:(j + 1) * 128]
    loads[4].wait()
    low = lax.broadcasted_iota(jnp.int32, (ROWS, 128), 1) < ROPE
    for h in range(HEADS):
        q = qr[:, (h // 2) * 128:(h // 2 + 1) * 128].astype(F32)
        qs[LANES, pl.ds(h, ROWS, stride=HEADS), :] = jnp.where(low if h % 2 == 0 else ~low, q, 0.0)

    def wait_par(i, _):
        src = lax.rem(me + i, GROUPS)
        remote(my_par, all_par.at[src], par_send.at[i], par_recv.at[src], branch=src).wait()
        return 0

    lax.fori_loop(1, GROUPS, wait_par, 0)
    local = all_par[...] - me * B_DEV
    hit = (local >= 0) & (local < B_DEV)
    pick_v[...] = jnp.broadcast_to(
        jnp.sum(jnp.where(hit, local, 0), axis=2, keepdims=True), (GROUPS, 1, 128)
    )
    pick = pltpu.make_async_copy(pick_v, pick_s, pick_sem)
    pick.start()
    loads[1].wait()

    @pl.when(core == 0)
    def _():
        extra().wait()

    pick.wait()

    def block(n, at, to, size):
        return remote(
            packed.at[n, pl.ds(0, size)], slots.at[at, pl.ds(0, size)], out_send.at[n], out_recv.at[at], branch=to
        )

    for c in range(2):

        @pl.when(core == c)
        def _(c=c):
            def send_block(i, _):
                d = lax.rem(me + i, GROUPS)
                packed[d] = mine[pick_s[d, 0, 0]]
                block(d, me, d, SIZES[c]).start()
                return 0

            lax.fori_loop(1, GROUPS, send_block, 0)

    slots[me] = mine[pick_s[me, 0, 0]]

    for i in range(2 * NX):
        wt[i * PADDED + SLICE:(i + 1) * PADDED, :] = jnp.zeros((PADDED - SLICE, HEADS * VDIM), BF)
    loads[10].wait()
    loads[11].wait()

    def share(m, owner, n, to):
        return remote(columns(owner, n), columns(owner, n), w_send.at[m], w_recv.at[m], branch=z * NX + to)

    for n in range(2):
        share(n, x, n, right).start()
        share(2 + n, x, n, left).start()

    for n in (5, 6, 7, 8):
        loads[n].wait()
    nlt[...] = jnp.zeros_like(nlt)
    nlt[:, :ROWS] = nl[...].astype(F32).T.astype(BF)

    key = lax.broadcasted_iota(jnp.int32, (STEPS * HEADS, 256), 1)
    step = lax.broadcasted_iota(jnp.int32, (STEPS * HEADS, 256), 0) // HEADS

    def query(rows):
        return jnp.concatenate([qs[j, rows, :] for j in range(LANES + 1)], axis=1).astype(BF)

    def scores(rows, keys):
        return dot(query(rows), jnp.concatenate([keys, keys[LAT:]], axis=0))

    def prefix(b, _):
        rows = pl.ds(pl.multiple_of(b * 64, 64), 64)
        keys = jnp.concatenate([pool[table[b]], nlt[...]], axis=1)
        s = scores(rows, keys)
        fresh = key - BLOCK - b * STEPS
        allowed = (key < lens[b]) | ((fresh >= 0) & (fresh <= step))
        s = jnp.where(allowed, s * SCALE, -jnp.inf)
        m = jnp.max(s, axis=1, keepdims=True)
        w = jnp.exp(s - m).astype(BF)
        total[rows, :] = jnp.broadcast_to(jnp.sum(w.astype(F32), axis=1, keepdims=True), (64, 128))
        peak[rows, :] = jnp.broadcast_to(m, (64, 128))
        c = dot_nt(w, keys[:LAT])
        for j in range(LANES):
            ctx[j, rows, :] = c[:, j * 128:(j + 1) * 128]
        return 0

    lax.fori_loop(0, EARLY, prefix, 0)

    from_down, from_up, from_far = down * 2 + core, up * 2 + core, far * 2 + core
    other = 1 - core

    def piece(h, ch, size, half):
        first, count = (ch * CHUNK, CHUNK) if half is None else (ch * CHUNK + half * (CHUNK // 2), CHUNK // 2)
        return parts.at[h, pl.ds(first, count), pl.ds(0, size)]

    def ring(n, h, ch, size, half, to):
        at = piece(h, ch, size, half)
        return remote(at, at, ring_send.at[ch, n], ring_recv.at[ch, n], head=to * 2 + core)

    def swap(n, h, ch, size, half):
        at = piece(h, ch, size, half)
        return remote(at, at, core_send.at[ch, n], core_recv.at[ch, n], head=y * 2 + other)

    def ring_first(ch, size):
        ring(0, head, ch, size, None, up).start()
        ring(1, head, ch, size, None, down).start()
        swap(0, head, ch, size, None).start()

    def ring_second(ch, size):
        ring(0, from_down, ch, size, None, up).wait()
        ring(2, from_down, ch, size, 0, up).start()
        ring(1, from_up, ch, size, None, down).wait()
        ring(3, from_up, ch, size, 1, down).start()
        swap(1, from_down, ch, size, None).start()
        swap(2, from_up, ch, size, None).start()

    def ring_third(ch, size):
        ring(2, from_far, ch, size, 0, up).wait()
        swap(3, from_far, ch, size, 0).start()
        ring(3, from_far, ch, size, 1, down).wait()
        swap(4, from_far, ch, size, 1).start()

    def ring_end(ch, size, other_size):
        for n, h, half in ((0, head, None), (1, from_down, None), (2, from_up, None), (3, from_far, 0), (4, from_far, 1)):
            swap(n, h, ch, size, half).wait_send()
            swap(n, h + other - core, ch, other_size, half).wait_recv()

    for c in range(2):

        @pl.when(core == c)
        def _(c=c):
            def wait_block(i, _):
                src = lax.rem(me + i, GROUPS)
                block(src, src, src, SIZES[c]).wait()
                return 0

            lax.fori_loop(1, GROUPS, wait_block, 0)
            for ch in range(2):
                for p in range(ch * CHUNK, (ch + 1) * CHUNK):
                    parts[head, p] = slots[par[2 * p] // B_DEV]
                ring_first(ch, SIZES[c])

    lax.fori_loop(EARLY, B_DEV, prefix, 0)

    for c in range(2):

        @pl.when(core == c)
        def _(c=c):
            ring_second(0, SIZES[c])
            ring_second(1, SIZES[c])
            ring_third(0, SIZES[c])
            ring_third(1, SIZES[c])

    share(0, left, 0, right).wait()
    share(4, left, 0, right).start()
    share(3, right, 1, left).wait()
    share(5, right, 1, left).start()
    share(1, left, 1, right).wait()
    share(2, right, 0, left).wait()

    def arrive(ch):
        for c in range(2):

            @pl.when(core == c)
            def _(c=c):
                ring_end(ch, SIZES[c], SIZES[1 - c])

        def gather(p, _):
            for yy in range(NY):
                fork[p, yy * 144:yy * 144 + 80] = parts[2 * yy, p]
                fork[p, yy * 144 + 80:yy * 144 + 144] = parts[2 * yy + 1, p, :64]
            return 0

        lax.fori_loop(ch * CHUNK, (ch + 1) * CHUNK, gather, 0)

    def forked(n, _):
        several = range(TOGETHER)
        rows = [pl.ds(pl.multiple_of((n * TOGETHER + i) * 128, 128), 128) for i in several]
        keys = [fork[n * TOGETHER + i] for i in several]
        s = [scores(rows[i], keys[i]) * SCALE for i in several]
        old = [peak[rows[i], :][:, :1] for i in several]
        m = [jnp.maximum(jnp.max(s[i], axis=1, keepdims=True), old[i]) for i in several]
        w = [jnp.exp(s[i] - m[i]).astype(BF) for i in several]
        back = [jnp.exp(old[i] - m[i]) for i in several]
        norm = [
            total[rows[i], :][:, :1] * back[i] + jnp.sum(w[i].astype(F32), axis=1, keepdims=True) for i in several
        ]
        c = [dot_nt(w[i], keys[i][:LAT]) for i in several]
        scale = [1.0 / norm[i] for i in several]
        both = [
            [(ctx[j, rows[i], :] * back[i] + c[i][:, j * 128:(j + 1) * 128]) * scale[i] for j in range(LANES)]
            for i in several
        ]
        for i in several:
            for j in range(LANES):
                ctx[j, rows[i], :] = both[i][j].astype(BF).astype(F32)
        return 0

    def half_of(slot, s):
        return held.at[slot, pl.ds(s * HALF, HALF)]

    def hop(way, k, s):
        came, goes = (k - 1, k) if way == 0 else ((9 - k) % 8, 8 - k)
        return remote(
            half_of(came, s), half_of(goes, s), z_send.at[way, k - 1, s], z_recv.at[way, k - 1, s],
            branch=nxt if way == 0 else prv,
        )

    hops = []

    def go(way, k, s):
        c = hop(way, k, s)
        c.start()
        hops.append(c)

    loads[9].wait()
    for s in (0, 1):
        arrive(s)
        lax.fori_loop(s * (PAIRS // 2) // TOGETHER, (s + 1) * (PAIRS // 2) // TOGETHER, forked, 0)
        for h in range(HEADS):
            c = [ctx[j, pl.ds(s * HALF * HEADS + h, HALF, stride=HEADS), :] for j in range(LANES)]
            c = jnp.concatenate(c, axis=1).astype(BF)
            held[0, s * HALF:(s + 1) * HALF, h * VDIM:(h + 1) * VDIM] = dot(c, vu[h]).astype(BF)
        go(0, 1, s)
        go(1, 1, s)

    share(4, lax.rem(x + 2, NX), 0, right).wait()
    share(5, lax.rem(x + 2, NX), 1, left).wait()

    def swap_sums(slot):
        return remote(made.at[slot, other], met.at[slot], r_send.at[slot], r_recv.at[slot], head=y * 2 + other)

    def multiply(slot):
        for i in range(NX):
            r = dot_nt(held[slot], wt[i * 2 * PADDED:(i + 1) * 2 * PADDED]).astype(BF)
            for n in range(2):
                made[slot, n, i] = r[:, n * PADDED:(n + 1) * PADDED]
        swap_sums(slot).start()

    def deliver(slot, i):
        return remote(
            summed.at[slot, i], landed.at[x, head], f_send.at[slot, i], f_recv.at[x, head],
            branch=z * NX + i, head=lax.rem(z + 8 - slot, 8),
        )

    def stays(slot, i):
        return (i == x) & (lax.rem(z + 8 - slot, 8) == head)

    def fold(slot):
        swap_sums(slot).wait_recv()
        for i in range(NX):
            both = (made[slot, core, i].astype(F32) + met[slot, i].astype(F32)).astype(BF)
            summed[slot, i] = both
            here = stays(slot, i)

            @pl.when(here)
            def _(both=both):
                landed[x, head] = both

            @pl.when(~here)
            def _(i=i):
                deliver(slot, i).start()

    order = (0, 1, 7, 2, 6, 3, 5, 4)

    def turn(slot):
        n = order.index(slot)
        multiply(slot)
        if 1 <= n < 7:
            fold(order[n - 1])

    turn(0)
    for k in (1, 2, 3):
        for s in (0, 1):
            for way in (0, 1):
                t = s if way == 0 else 1 - s
                hop(way, k, t).wait_recv()
                if k < 3 or t == way:
                    go(way, k + 1, t)
            if s == 0 and k > 1:
                turn(9 - k)
        turn(k)
    turn(5)
    fold(5)
    hop(0, 4, 0).wait_recv()
    hop(1, 4, 1).wait_recv()
    turn(4)
    fold(4)

    for i in range(NX):
        sides = []
        for n in range(2):
            acc = jnp.zeros((ROWS, PADDED), F32)
            for yy in range(NY):
                src = 2 * yy + n

                @pl.when((i != x) | (src != head))
                def _(i=i, src=src):
                    remote(
                        summed.at[0, 0], landed.at[i, src], f_send.at[0, 0], f_recv.at[i, src],
                        branch=z * NX + i, head=src,
                    ).wait_recv()

                acc = acc + landed[i, src].astype(F32)
            sides.append(acc.astype(BF)[:, :SLICE])
        out[i * ROWS:(i + 1) * ROWS, :] = jnp.concatenate(sides, axis=1)

    for c in hops:
        c.wait_send()
    for slot in range(8):
        swap_sums(slot).wait_send()
        for i in range(NX):

            @pl.when(~stays(slot, i))
            def _(slot=slot, i=i):
                deliver(slot, i).wait_send()


def layer(*operands):
    vmem, dma = pltpu.VMEM, pltpu.SemaphoreType.DMA
    smem = pltpu.SMEM
    return pl.pallas_call(
        layer_kernel,
        out_shape=jax.ShapeDtypeStruct((NX * ROWS, COLS), BF),
        in_specs=[pl.BlockSpec(memory_space=pl.ANY)] * 11,
        out_specs=pl.BlockSpec(memory_space=pltpu.VMEM),
        scratch_shapes=[
            smem((B_DEV,), jnp.int32), smem((B_DEV,), jnp.int32), smem((B_DEV,), jnp.int32),
            vmem((ROWS, HEADS * NOPE), BF),
            vmem((ROWS, HEADS * ROPE), BF),
            vmem((HEADS, NOPE, LAT), BF),
            vmem((HEADS, LAT, VDIM), BF),
            vmem((B_DEV, WIDTH, BLOCK), BF),
            vmem((ROWS, WIDTH), BF),
            vmem((WIDTH, 128), BF),
            vmem((2 * NX * PADDED, HEADS * VDIM), BF),
            vmem((LANES + 1, QROWS, 128), F32),
            vmem((LANES, QROWS, 128), F32),
            vmem((QROWS, 128), F32),
            vmem((QROWS, 128), F32),
            vmem((B_DEV, PART, 128), BF),
            vmem((GROUPS, PART, 128), BF),
            vmem((GROUPS, PART, 128), BF),
            vmem((1, 128), jnp.int32),
            vmem((GROUPS, 1, 128), jnp.int32),
            vmem((GROUPS, 1, 128), jnp.int32),
            smem((GROUPS, 1, 128), jnp.int32),
            vmem((8, PAIRS, PART, 128), BF),
            vmem((PAIRS, WIDTH, BLOCK), BF),
            vmem((8, ROWS, HEADS * VDIM), BF),
            vmem((8, 2, NY, ROWS, PADDED), BF),
            vmem((8, NX, ROWS, PADDED), BF),
            vmem((8, NX, ROWS, PADDED), BF),
            vmem((NX, 8, ROWS, PADDED), BF),
            dma((13,)), dma,
            dma((GROUPS,)), dma((GROUPS,)), dma((GROUPS,)), dma((GROUPS,)),
            dma((2, 4)), dma((2, 4)), dma((2, 5)), dma((2, 5)),
            dma((6,)), dma((6,)), dma((2, 4, 2)), dma((2, 4, 2)), dma((8,)), dma((8,)), dma((8, NX)), dma((NX, 8)),
        ],
        compiler_params=pltpu.CompilerParams(
            collective_id=0, has_side_effects=True, vmem_limit_bytes=VMEM_BYTES
        ),
        cost_estimate=pl.CostEstimate(flops=4_200_000_000, bytes_accessed=16_000_000, transcendentals=400_000),
    )(*operands)


def local(
    query_nope, query_rope, key_up, value_up, out_weight, block_pool, recent_blocks, new_latent,
    parent, lengths, block_table,
):
    return layer(
        parent, lengths, block_table.reshape(B_DEV), query_nope, query_rope, key_up, value_up,
        jnp.swapaxes(block_pool, 1, 2), jnp.swapaxes(recent_blocks, 1, 2), new_latent, out_weight.T,
    )


def solution(mesh):
    return jax.shard_map(
        local,
        mesh=mesh,
        in_specs=(
            P("branch", "head"),
            P("branch", "head"),
            P("head", None, None),
            P("head", None, None),
            P("head", "branch"),
            P("branch", None, None),
            P("branch", None, None),
            P("branch", None),
            P("branch"),
            P("branch"),
            P("branch", None),
        ),
        out_specs=P("head", "branch"),
        check_vma=False,
    )
```
